32 devices in a mesh: groups: 2 (over y), tok: 8 (over z, x), head: 2 (over core).
Axes of the slice: x: 2, y: 2, z: 4, core: 2. Of those that a mesh axis runs over, the one named last changes fastest.
Arguments:
- interior_element_embedding: bfloat16 [2048, 1024], P(('groups', 'tok')), parts along dimension 0, may hold values from -70 to 70
- boundary_element_embedding: bfloat16 [512, 1024], P(('groups', 'tok')), parts along dimension 0, may hold values from -70 to 70
- interior_landmark_position: int32 [256], P(('groups', 'tok')), parts along dimension 0, may hold values from 0 to 1023, as said below
- boundary_landmark_position: int32 [128], P(('groups', 'tok')), parts along dimension 0, may hold values from 0 to 255, as said below
- interior_rescaling_factor: float32 [1024], replicated, may hold values from 0.1 to 1.9
- boundary_rescaling_factor: float32 [1024], replicated, may hold values from 0.1 to 1.9
- question_projection_matrix: bfloat16 [1024, 1024], P(None, 'head'), may hold values from -0.1875 to 0.1875
- lookup_projection_matrix: bfloat16 [1024, 1024], P(None, 'head'), may hold values from -0.1875 to 0.1875
- content_projection_matrix: bfloat16 [1024, 1024], P(None, 'head'), may hold values from -0.1875 to 0.1875
- final_projection_matrix: bfloat16 [1024, 1024], P('head'), may hold values from -0.1875 to 0.1875
- channel_logit_divisor: float32 [16], P('head'), may hold values from 0.5 to 96
Outputs:
- update: bfloat16 [2048, 1024], P(('groups', 'tok'), 'head'), parts along dimension 0
The draws below stay inside these ranges and needn't reach their ends.
There are 2 independent parts, one for each index of `groups`. The reference program is written for one: setup_inputs(seed, part) draws one part's arguments, and reference() takes and returns one part's arrays. A program takes and returns all parts, laid end to end along the dimension named above; an argument that names none is the same for every part. Nothing has to cross between parts.
Inputs may be any that keep to these rules, and one draw needn't show every extreme that they name: `interior_landmark_position`: anchor i lies among the 128 cells of block i // 16, that is from (i // 16) * 128 on; no cell is named twice; cell 0 and the last cell of the last block are always anchors. `boundary_landmark_position`: anchor i lies among the 32 cells of block i // 8, that is from (i // 8) * 32 on; no cell is named twice; cell 0 and the last cell of the last block are always anchors.
All inputs are finite; a program needn't handle non-finite values.
Results may differ from the reference program's by a relative error of at most 0.012.
The reference program's roundings to bfloat16 on the way (of `vol_normed`, `surf_normed`, `anchors`, `queries`, `anchor_keys`, `anchor_values`, `rounded` and `context`) count: a program that leaves them out, or rounds other values in their place, can miss the bound.
Values may be sent and summed in bfloat16 or wider, within the bound.
No kernel may reach another device: no remote copies, remote signals or barrier semaphores. Data moves between devices by JAX's collectives and lax.ppermute only.
A program may use at most 64 MiB of HBM per device.

```python
import math
import jax
import jax.numpy as jnp
from jax import lax

D = 1024
HEADS = 16
CV_DEV = 128
VA_DEV = 16
SA_DEV = 8
CS_DEV = 32
VCELLS = 1024
SCELLS = 256
VA = 128
SA = 64


def scaled_cells(key, row_count):
    subkeys = jax.random.split(key, 3)
    entries = jnp.clip(jax.random.normal(subkeys[0], (row_count, D), jnp.float32), -4.0, 4.0)
    row_scale = jnp.exp(jax.random.uniform(subkeys[2], (row_count, 1), jnp.float32, 0.0, math.log(10.0)))
    column_scale = jnp.exp(jax.random.uniform(subkeys[1], (1, D), jnp.float32, 0.0, math.log(10.0)))
    return (entries * row_scale * column_scale * 0.1).astype(jnp.bfloat16)


def pick_cells(key, block_count, per_block, picks):
    block_keys = jax.random.split(key, block_count)

    def one_block(block_key, block_number):
        drawn_pick = jax.random.permutation(block_key, per_block)[:picks].astype(jnp.int32)
        narrow = jax.random.permutation(block_key, per_block - 1)[:picks].astype(jnp.int32)
        first_block = jnp.concatenate([jnp.zeros((1,), jnp.int32), narrow[1:] + 1])
        last_block = jnp.concatenate([jnp.full((1,), per_block - 1, jnp.int32), narrow[1:]])
        chosen = jnp.where(block_number == 0, first_block, jnp.where(block_number == block_count - 1, last_block, drawn_pick))
        return chosen + block_number * per_block
    return jax.vmap(one_block)(block_keys, jnp.arange(block_count, dtype=jnp.int32)).reshape(-1)


def draw_interior_element_embedding(key, part):
    return scaled_cells(jax.random.fold_in(key, 11), VCELLS)


def draw_boundary_element_embedding(key, part):
    return scaled_cells(jax.random.fold_in(key, 12), SCELLS)


def draw_interior_landmark_position(key, part):
    return pick_cells(jax.random.fold_in(key, 21), VA // VA_DEV, CV_DEV, VA_DEV)


def draw_boundary_landmark_position(key, part):
    return pick_cells(jax.random.fold_in(key, 22), SA // SA_DEV, CS_DEV, SA_DEV)


def draw_channel_logit_divisor(key, part):
    subkeys = jax.random.split(jax.random.fold_in(key, 31), 1)
    return jnp.exp(jax.random.uniform(subkeys[0], (HEADS,), jnp.float32, math.log(0.5), math.log(2.0)))


def shard_levels(rng, extent, shards, least, high):
    factor_of, own = 1.0, jax.random.fold_in(rng, 6)
    for position, blocks in shards:
        heights = jnp.exp(jax.random.uniform(jax.random.fold_in(own, position), (blocks,), jnp.float32, least / len(shards), high / len(shards)))
        factor_of = factor_of * jnp.repeat(heights, extent[position] // blocks).reshape([-1 if axis == position else 1 for axis in range(len(extent))])
    return factor_of


def noise(key, shape, width, limit, shards=(), kind=jnp.bfloat16):
    values = width * jax.random.normal(key, shape, jnp.float32)
    if shards:
        values = values * shard_levels(key, shape, shards, -0.22, 0.18)
    return jnp.clip(values, -limit, limit).astype(kind)


def setup_inputs(seed: int = 0, part: int = 0) -> dict:
    key_of = jax.random.split(jax.random.key(seed), 12)
    part_splits = jax.random.split(jax.random.fold_in(key_of[11], part), 12)
    interior_element_embedding = draw_interior_element_embedding(jax.random.fold_in(jax.random.fold_in(key_of[11], part), 71), part)
    boundary_element_embedding = draw_boundary_element_embedding(jax.random.fold_in(jax.random.fold_in(key_of[11], part), 71), part)
    interior_landmark_position = draw_interior_landmark_position(jax.random.fold_in(jax.random.fold_in(key_of[11], part), 71), part)
    boundary_landmark_position = draw_boundary_landmark_position(jax.random.fold_in(jax.random.fold_in(key_of[11], part), 71), part)
    interior_rescaling_factor = jnp.clip(1.0 + 0.18 * jax.random.normal(key_of[4], (D,), jnp.float32), 0.1, 1.9)
    boundary_rescaling_factor = jnp.clip(1.0 + 0.18 * jax.random.normal(key_of[5], (D,), jnp.float32), 0.1, 1.9)
    question_projection_matrix = noise(key_of[6], (D, D), D ** -0.5, 0.1875, ((1, 2),))
    lookup_projection_matrix = noise(key_of[7], (D, D), D ** -0.5, 0.1875, ((1, 2),))
    content_projection_matrix = noise(key_of[8], (D, D), D ** -0.5, 0.1875, ((1, 2),))
    final_projection_matrix = noise(key_of[9], (D, D), D ** -0.5, 0.1875, ((0, 2),))
    channel_logit_divisor = draw_channel_logit_divisor(jax.random.fold_in(key_of[11], 71), part)
    return {"interior_element_embedding": interior_element_embedding, "boundary_element_embedding": boundary_element_embedding, "interior_landmark_position": interior_landmark_position, "boundary_landmark_position": boundary_landmark_position, "interior_rescaling_factor": interior_rescaling_factor, "boundary_rescaling_factor": boundary_rescaling_factor, "question_projection_matrix": question_projection_matrix, "lookup_projection_matrix": lookup_projection_matrix, "content_projection_matrix": content_projection_matrix, "final_projection_matrix": final_projection_matrix, "channel_logit_divisor": channel_logit_divisor}


epsilon = 1e-06

def rms_rows(cells, gain):
    values = cells.astype(jnp.float32)
    mean_square = lax.optimization_barrier(jnp.mean(values * values, axis=1, keepdims=True))
    return (values * lax.rsqrt(mean_square + epsilon) * gain).astype(jnp.bfloat16)

def reference(interior_element_embedding, boundary_element_embedding, interior_landmark_position, boundary_landmark_position, interior_rescaling_factor, boundary_rescaling_factor, question_projection_matrix, lookup_projection_matrix, content_projection_matrix, final_projection_matrix, channel_logit_divisor):
    vol_normed = rms_rows(interior_element_embedding, interior_rescaling_factor)
    surf_normed = rms_rows(jnp.take(boundary_element_embedding, boundary_landmark_position.astype(jnp.int32), axis=0), boundary_rescaling_factor)
    anchors = jnp.concatenate([jnp.take(vol_normed, interior_landmark_position.astype(jnp.int32), axis=0), surf_normed], axis=0)
    queries = jnp.dot(vol_normed, question_projection_matrix, preferred_element_type=jnp.float32).astype(jnp.bfloat16)
    anchor_keys = jnp.dot(anchors, lookup_projection_matrix, preferred_element_type=jnp.float32).astype(jnp.bfloat16)
    anchor_values = jnp.dot(anchors, content_projection_matrix, preferred_element_type=jnp.float32).astype(jnp.bfloat16)
    channel_dimension = D // HEADS
    key_heads = anchor_keys.astype(jnp.float32).reshape(-1, HEADS, channel_dimension)
    value_heads = anchor_values.astype(jnp.float32).reshape(-1, HEADS, channel_dimension)
    logit_multiplier = channel_logit_divisor * (1.0 / math.sqrt(channel_dimension))
    block_rows = math.gcd(VCELLS, 512)
    query_blocks = queries.reshape(VCELLS // block_rows, block_rows, HEADS, channel_dimension)

    def attend(query_block):
        scores = jnp.einsum('qhd,khd->hqk', query_block.astype(jnp.float32), key_heads) * logit_multiplier[:, None, None]
        row_max = lax.optimization_barrier(jnp.max(scores, axis=2, keepdims=True))
        exp_scores = jnp.exp(scores - row_max)
        denominator = lax.optimization_barrier(jnp.sum(exp_scores, axis=2))
        rounded = lax.optimization_barrier(exp_scores.astype(jnp.bfloat16)).astype(jnp.float32)
        accumulated = jnp.einsum('hqk,khd->qhd', rounded, value_heads)
        context = accumulated / jnp.transpose(denominator)[:, :, None]
        return context.reshape(query_block.shape[0], D).astype(jnp.bfloat16)
    context = lax.map(attend, query_blocks).reshape(VCELLS, D)
    mixed_rows = jnp.dot(context, final_projection_matrix, preferred_element_type=jnp.float32)
    mean_square = lax.optimization_barrier(jnp.mean(mixed_rows * mixed_rows, axis=1, keepdims=True))
    return (mixed_rows * lax.rsqrt(mean_square + epsilon)).astype(jnp.bfloat16)
```

```python
import functools
import math

import jax
import jax.numpy as jnp
from jax import lax
from jax.experimental import pallas as pl
from jax.experimental.pallas import tpu as pltpu
from jax.sharding import PartitionSpec as P

epsilon = 1e-06
key_block = 512


def rms_rows(cells, gain):
    values = cells.astype(jnp.float32)
    mean_square = jnp.mean(values * values, axis=1, keepdims=True)
    return (values * lax.rsqrt(mean_square + epsilon) * gain).astype(jnp.bfloat16)


def absorb(running, key_rows, value_rows, queries, logit_multiplier):
    run_max, denominator, accumulated = running
    parallel_channel_total, channel_dimension, cell_count = queries.shape
    key_heads = key_rows.reshape(key_rows.shape[0], parallel_channel_total, channel_dimension)
    value_heads = value_rows.reshape(value_rows.shape[0], parallel_channel_total, channel_dimension)
    scores = (
        jnp.einsum("jhd,hdc->hjc", key_heads, queries, preferred_element_type=jnp.float32)
        * logit_multiplier
    )
    new_max = jnp.maximum(run_max, jnp.max(scores, axis=1))
    shrink = jnp.exp(run_max - new_max)
    exp_scores = jnp.exp(scores - new_max[:, None, :])
    denominator = denominator * shrink + jnp.sum(exp_scores, axis=1)
    added = jnp.einsum(
        "jhd,hjc->hdc",
        value_heads,
        exp_scores.astype(jnp.bfloat16),
        preferred_element_type=jnp.float32,
    )
    accumulated = accumulated * shrink[:, None, :] + added
    return (new_max, denominator, accumulated)


def make_folder(queries, logit_multiplier):

    def folder(running, shard_rows, offset):
        key_rows, value_rows = shard_rows
        row_count = key_rows.shape[0]
        if row_count > key_block and row_count % key_block == 0:
            row_width = key_rows.shape[1]

            def scan_step(state, key_pair):
                return (absorb(state, key_pair[0], key_pair[1], queries, logit_multiplier), None)

            stacked = (
                key_rows.reshape(row_count // key_block, key_block, row_width),
                value_rows.reshape(row_count // key_block, key_block, row_width),
            )
            running, unused = lax.scan(scan_step, running, stacked)
            return running
        return absorb(running, key_rows, value_rows, queries, logit_multiplier)

    return folder


def project_pair(rows_in, lookup_projection_matrix, content_projection_matrix):
    key_rows = jnp.dot(
        rows_in, lookup_projection_matrix, preferred_element_type=jnp.float32
    ).astype(jnp.bfloat16)
    value_rows = jnp.dot(
        rows_in, content_projection_matrix, preferred_element_type=jnp.float32
    ).astype(jnp.bfloat16)
    return (key_rows, value_rows)


def gathered_body(
    interior_element_embedding,
    boundary_element_embedding,
    interior_landmark_position,
    boundary_landmark_position,
    interior_rescaling_factor,
    boundary_rescaling_factor,
    question_projection_matrix,
    lookup_projection_matrix,
    content_projection_matrix,
    final_projection_matrix,
    channel_logit_divisor,
):
    block_index = lax.axis_index("tok")
    vol_normed = rms_rows(interior_element_embedding, interior_rescaling_factor)
    vol_local = interior_landmark_position - block_index * interior_element_embedding.shape[0]
    surf_local = boundary_landmark_position - block_index * boundary_element_embedding.shape[0]
    vol_picked = jnp.take(vol_normed, vol_local, axis=0)
    surf_picked = rms_rows(
        jnp.take(boundary_element_embedding, surf_local, axis=0), boundary_rescaling_factor
    )
    parallel_channel_total = channel_logit_divisor.shape[0]
    local_width = question_projection_matrix.shape[1]
    channel_dimension = local_width // parallel_channel_total
    cell_count = interior_element_embedding.shape[0]
    query_cols = lax.dot_general(
        question_projection_matrix,
        vol_normed,
        (((0,), (1,)), ((), ())),
        preferred_element_type=jnp.float32,
    )
    queries = query_cols.astype(jnp.bfloat16).reshape(
        parallel_channel_total, channel_dimension, cell_count
    )
    logit_multiplier = (channel_logit_divisor * (1.0 / math.sqrt(channel_dimension)))[:, None, None]
    start_state = (
        jnp.full((parallel_channel_total, cell_count), -1e30, jnp.float32),
        jnp.zeros((parallel_channel_total, cell_count), jnp.float32),
        jnp.zeros((parallel_channel_total, channel_dimension, cell_count), jnp.float32),
    )
    folder = make_folder(queries, logit_multiplier)
    anchors = jnp.concatenate([vol_picked, surf_picked], axis=0)
    anchor_keys, anchor_values = project_pair(
        anchors, lookup_projection_matrix, content_projection_matrix
    )
    final_state = folder(
        start_state,
        (
            lax.all_gather(anchor_keys, "tok", axis=0, tiled=True),
            lax.all_gather(anchor_values, "tok", axis=0, tiled=True),
        ),
        jnp.int32(0),
    )
    run_max, denominator, accumulated = final_state
    context = (
        (accumulated / denominator[:, None, :])
        .astype(jnp.bfloat16)
        .reshape(local_width, cell_count)
    )
    head_terms = lax.dot_general(
        context,
        final_projection_matrix,
        (((0,), (0,)), ((), ())),
        preferred_element_type=jnp.float32,
    )
    full_width = head_terms.shape[1]
    share = lax.psum_scatter(
        head_terms.astype(jnp.bfloat16), "head", scatter_dimension=1, tiled=True
    ).astype(jnp.float32)
    squares = lax.psum(jnp.sum(share * share, axis=1), "head")
    return (share * lax.rsqrt(squares[:, None] / full_width + epsilon)).astype(jnp.bfloat16)


def in_vmem(array):
    return pltpu.with_memory_space_constraint(array, pltpu.VMEM)


def normed(values, gain):
    mean_square = jnp.mean(values * values, axis=1, keepdims=True)
    return (values * lax.rsqrt(mean_square + epsilon) * gain).astype(jnp.bfloat16)


def pick_rows(positions, first, cells):
    picks, rows = positions.shape[0], cells.shape[0]
    row = lax.broadcasted_iota(jnp.int32, (picks, rows), 0)
    column = lax.broadcasted_iota(jnp.int32, (picks, rows), 1)
    chosen = jnp.zeros((picks, rows), jnp.int32)
    for pick in range(picks):
        chosen = jnp.where(row == pick, positions[pick] - first, chosen)
    one_hot = jnp.where(chosen == column, 1.0, 0.0).astype(jnp.bfloat16)
    return jnp.dot(one_hot, cells, preferred_element_type=jnp.float32)


def anchor_kernel(vol_position, surf_position, vol, surf, vol_gain, surf_gain, anchors):
    block_index = lax.axis_index("tok")
    vol_rows = pick_rows(vol_position, block_index * vol.shape[0], vol[...])
    surf_rows = pick_rows(surf_position, block_index * surf.shape[0], surf[...])
    parts = [normed(vol_rows, vol_gain[...]), normed(surf_rows, surf_gain[...])]
    stacked = jnp.concatenate([part.astype(jnp.float32) for part in parts], axis=0)
    anchors[...] = stacked.astype(jnp.bfloat16)


def query_kernel(vol, gain, projection, value_projection, queries, value_turned):
    vol_normed = normed(vol[...].astype(jnp.float32), gain[...])
    cells = vol.shape[0]
    columns = lax.dot_general(
        projection[...], vol_normed, (((0,), (1,)), ((), ())), preferred_element_type=jnp.float32
    ).astype(jnp.bfloat16)
    pairs, pair_width, _ = queries.shape
    half = pair_width // 2
    upper = lax.broadcasted_iota(jnp.int32, (pair_width, cells), 0) < half
    for pair in range(pairs):
        block = columns[pair * pair_width : (pair + 1) * pair_width, :].astype(jnp.float32)
        queries[pair, :, :cells] = jnp.where(upper, block, 0.0).astype(jnp.bfloat16)
        queries[pair, :, cells:] = jnp.where(upper, 0.0, block).astype(jnp.bfloat16)
    value_turned[...] = value_projection[...].T


def attention_kernel(block_count, divisor, queries, lookup, value_turned, final, *rest):
    blocks, terms, context = rest[:block_count], rest[block_count], rest[block_count + 1]
    pairs, pair_width, wide = queries.shape
    half, cells = pair_width // 2, wide // 2
    rows = [block[...].astype(jnp.float32) for block in blocks[:-2]]
    rows.append(blocks[-2][...].astype(jnp.float32) + blocks[-1][...].astype(jnp.float32))
    anchors = jnp.concatenate(rows, axis=0).astype(jnp.bfloat16)
    keys = jnp.dot(anchors, lookup[...], preferred_element_type=jnp.float32).astype(jnp.bfloat16)
    values = lax.dot_general(
        value_turned[...], anchors, (((1,), (1,)), ((), ())), preferred_element_type=jnp.float32
    ).astype(jnp.bfloat16)
    left = lax.broadcasted_iota(jnp.int32, (1, wide), 1) < cells
    scale = 1.0 / math.sqrt(half)
    for pair in range(pairs):
        span = slice(pair * pair_width, (pair + 1) * pair_width)
        multiplier = jnp.where(left, divisor[2 * pair] * scale, divisor[2 * pair + 1] * scale)
        scores = jnp.dot(keys[:, span], queries[pair], preferred_element_type=jnp.float32) * multiplier
        exp_scores = jnp.exp(scores - jnp.max(scores, axis=0, keepdims=True))
        denominator = jnp.sum(exp_scores, axis=0, keepdims=True)
        added = jnp.dot(
            values[span, :], exp_scores.astype(jnp.bfloat16), preferred_element_type=jnp.float32
        )
        added = added / denominator
        context[span, :] = jnp.concatenate(
            [added[:half, :cells], added[half:, cells:]], axis=0
        ).astype(jnp.bfloat16)
    terms[...] = lax.dot_general(
        context[...], final[...], (((0,), (0,)), ((), ())), preferred_element_type=jnp.float32
    ).astype(jnp.bfloat16)


def finish_kernel(own, other, update):
    mixed = own[...].astype(jnp.float32) + other[...].astype(jnp.float32)
    factor = lax.rsqrt(jnp.mean(mixed * mixed, axis=1, keepdims=True) + epsilon)
    width = update.shape[1]
    for part in range(mixed.shape[1] // width):

        @pl.when(lax.axis_index("head") == part)
        def _():
            update[...] = (mixed[:, part * width : (part + 1) * width] * factor).astype(update.dtype)


SMEM = pl.BlockSpec(memory_space=pltpu.SMEM)
VMEM = pl.BlockSpec(memory_space=pltpu.VMEM)
PARAMS = pltpu.CompilerParams(vmem_limit_bytes=32 * 1024 * 1024)


def direct_body(
    shards,
    interior_element_embedding,
    boundary_element_embedding,
    interior_landmark_position,
    boundary_landmark_position,
    interior_rescaling_factor,
    boundary_rescaling_factor,
    question_projection_matrix,
    lookup_projection_matrix,
    content_projection_matrix,
    final_projection_matrix,
    channel_logit_divisor,
):
    cells, width = interior_element_embedding.shape
    local_width = question_projection_matrix.shape[1]
    heads = channel_logit_divisor.shape[0]
    pair_width = 2 * (local_width // heads)
    picks = interior_landmark_position.shape[0] + boundary_landmark_position.shape[0]
    vol_gain = interior_rescaling_factor.reshape(1, width)
    surf_gain = boundary_rescaling_factor.reshape(1, width)
    anchors = pl.pallas_call(
        anchor_kernel,
        out_shape=jax.ShapeDtypeStruct((picks, width), jnp.bfloat16),
        in_specs=[SMEM, SMEM, VMEM, VMEM, VMEM, VMEM],
        out_specs=VMEM,
        compiler_params=PARAMS,
        name="anchors",
    )(
        interior_landmark_position,
        boundary_landmark_position,
        interior_element_embedding,
        boundary_element_embedding,
        vol_gain,
        surf_gain,
    )
    arrived = []
    for odd in range(1, shards, 2):
        pairs = [(2 * t, 2 * ((t + odd) % shards)) for t in range(shards)]
        if odd + 1 < shards:
            pairs += [(2 * t + 1, 2 * ((t + odd + 1) % shards) + 1) for t in range(shards)]
        arrived.append(lax.ppermute(anchors, ("tok", "head"), pairs))
    swapped = [lax.ppermute(block, "head", [(0, 1), (1, 0)]) for block in arrived[:-1]]
    swapped.append(lax.ppermute(arrived[-1], "head", [(0, 1)]))
    queries, value_turned = pl.pallas_call(
        query_kernel,
        out_shape=(
            jax.ShapeDtypeStruct((heads // 2, pair_width, 2 * cells), jnp.bfloat16),
            jax.ShapeDtypeStruct((local_width, width), jnp.bfloat16),
        ),
        in_specs=[VMEM] * 4,
        out_specs=(VMEM, VMEM),
        compiler_params=PARAMS,
        cost_estimate=pl.CostEstimate(
            flops=2 * cells * width * local_width, bytes_accessed=4 * width * local_width, transcendentals=0
        ),
        name="queries",
    )(
        interior_element_embedding,
        vol_gain,
        in_vmem(question_projection_matrix),
        in_vmem(content_projection_matrix),
    )
    blocks = [anchors, *arrived[:-1], *swapped[:-1], arrived[-1], swapped[-1]]
    terms = pl.pallas_call(
        functools.partial(attention_kernel, len(blocks)),
        out_shape=jax.ShapeDtypeStruct((cells, width), jnp.bfloat16),
        in_specs=[SMEM] + [VMEM] * (4 + len(blocks)),
        out_specs=VMEM,
        scratch_shapes=[pltpu.VMEM((local_width, cells), jnp.bfloat16)],
        compiler_params=PARAMS,
        name="attention",
    )(
        channel_logit_divisor,
        in_vmem(queries),
        in_vmem(lookup_projection_matrix),
        in_vmem(value_turned),
        in_vmem(final_projection_matrix),
        *[in_vmem(block) for block in blocks],
    )
    other = lax.ppermute(terms, "head", [(0, 1), (1, 0)])
    return pl.pallas_call(
        finish_kernel,
        out_shape=jax.ShapeDtypeStruct((cells, local_width), jnp.bfloat16),
        in_specs=[VMEM, VMEM],
        out_specs=VMEM,
        compiler_params=PARAMS,
        name="finish",
    )(in_vmem(terms), in_vmem(other))


def solution(mesh):
    placed = (
        P(("groups", "tok"), None),
        P(("groups", "tok"), None),
        P(("groups", "tok")),
        P(("groups", "tok")),
        P(),
        P(),
        P(None, "head"),
        P(None, "head"),
        P(None, "head"),
        P("head", None),
        P("head"),
    )
    shards = mesh.shape["tok"]
    small = shards % 2 == 0 and shards <= 16 and mesh.shape["head"] == 2
    body = functools.partial(direct_body, shards) if small else gathered_body
    return jax.shard_map(
        body, mesh=mesh, in_specs=placed, out_specs=P(("groups", "tok"), "head"), check_vma=False
    )
```

```python
import functools
import math

import jax
import jax.numpy as jnp
from jax import lax
from jax.experimental import pallas as pl
from jax.experimental.pallas import tpu as pltpu
from jax.sharding import PartitionSpec as P

epsilon = 1e-06
key_block = 512


def rms_rows(cells, gain):
    values = cells.astype(jnp.float32)
    mean_square = jnp.mean(values * values, axis=1, keepdims=True)
    return (values * lax.rsqrt(mean_square + epsilon) * gain).astype(jnp.bfloat16)


def absorb(running, key_rows, value_rows, queries, logit_multiplier):
    run_max, denominator, accumulated = running
    parallel_channel_total, channel_dimension, cell_count = queries.shape
    key_heads = key_rows.reshape(key_rows.shape[0], parallel_channel_total, channel_dimension)
    value_heads = value_rows.reshape(value_rows.shape[0], parallel_channel_total, channel_dimension)
    scores = (
        jnp.einsum("jhd,hdc->hjc", key_heads, queries, preferred_element_type=jnp.float32)
        * logit_multiplier
    )
    new_max = jnp.maximum(run_max, jnp.max(scores, axis=1))
    shrink = jnp.exp(run_max - new_max)
    exp_scores = jnp.exp(scores - new_max[:, None, :])
    denominator = denominator * shrink + jnp.sum(exp_scores, axis=1)
    added = jnp.einsum(
        "jhd,hjc->hdc",
        value_heads,
        exp_scores.astype(jnp.bfloat16),
        preferred_element_type=jnp.float32,
    )
    accumulated = accumulated * shrink[:, None, :] + added
    return (new_max, denominator, accumulated)


def make_folder(queries, logit_multiplier):

    def folder(running, shard_rows, offset):
        key_rows, value_rows = shard_rows
        row_count = key_rows.shape[0]
        if row_count > key_block and row_count % key_block == 0:
            row_width = key_rows.shape[1]

            def scan_step(state, key_pair):
                return (absorb(state, key_pair[0], key_pair[1], queries, logit_multiplier), None)

            stacked = (
                key_rows.reshape(row_count // key_block, key_block, row_width),
                value_rows.reshape(row_count // key_block, key_block, row_width),
            )
            running, unused = lax.scan(scan_step, running, stacked)
            return running
        return absorb(running, key_rows, value_rows, queries, logit_multiplier)

    return folder


def project_pair(rows_in, lookup_projection_matrix, content_projection_matrix):
    key_rows = jnp.dot(
        rows_in, lookup_projection_matrix, preferred_element_type=jnp.float32
    ).astype(jnp.bfloat16)
    value_rows = jnp.dot(
        rows_in, content_projection_matrix, preferred_element_type=jnp.float32
    ).astype(jnp.bfloat16)
    return (key_rows, value_rows)


def gathered_body(
    interior_element_embedding,
    boundary_element_embedding,
    interior_landmark_position,
    boundary_landmark_position,
    interior_rescaling_factor,
    boundary_rescaling_factor,
    question_projection_matrix,
    lookup_projection_matrix,
    content_projection_matrix,
    final_projection_matrix,
    channel_logit_divisor,
):
    block_index = lax.axis_index("tok")
    vol_normed = rms_rows(interior_element_embedding, interior_rescaling_factor)
    vol_local = interior_landmark_position - block_index * interior_element_embedding.shape[0]
    surf_local = boundary_landmark_position - block_index * boundary_element_embedding.shape[0]
    vol_picked = jnp.take(vol_normed, vol_local, axis=0)
    surf_picked = rms_rows(
        jnp.take(boundary_element_embedding, surf_local, axis=0), boundary_rescaling_factor
    )
    parallel_channel_total = channel_logit_divisor.shape[0]
    local_width = question_projection_matrix.shape[1]
    channel_dimension = local_width // parallel_channel_total
    cell_count = interior_element_embedding.shape[0]
    query_cols = lax.dot_general(
        question_projection_matrix,
        vol_normed,
        (((0,), (1,)), ((), ())),
        preferred_element_type=jnp.float32,
    )
    queries = query_cols.astype(jnp.bfloat16).reshape(
        parallel_channel_total, channel_dimension, cell_count
    )
    logit_multiplier = (channel_logit_divisor * (1.0 / math.sqrt(channel_dimension)))[:, None, None]
    start_state = (
        jnp.full((parallel_channel_total, cell_count), -1e30, jnp.float32),
        jnp.zeros((parallel_channel_total, cell_count), jnp.float32),
        jnp.zeros((parallel_channel_total, channel_dimension, cell_count), jnp.float32),
    )
    folder = make_folder(queries, logit_multiplier)
    anchors = jnp.concatenate([vol_picked, surf_picked], axis=0)
    anchor_keys, anchor_values = project_pair(
        anchors, lookup_projection_matrix, content_projection_matrix
    )
    final_state = folder(
        start_state,
        (
            lax.all_gather(anchor_keys, "tok", axis=0, tiled=True),
            lax.all_gather(anchor_values, "tok", axis=0, tiled=True),
        ),
        jnp.int32(0),
    )
    run_max, denominator, accumulated = final_state
    context = (
        (accumulated / denominator[:, None, :])
        .astype(jnp.bfloat16)
        .reshape(local_width, cell_count)
    )
    head_terms = lax.dot_general(
        context,
        final_projection_matrix,
        (((0,), (0,)), ((), ())),
        preferred_element_type=jnp.float32,
    )
    full_width = head_terms.shape[1]
    share = lax.psum_scatter(
        head_terms.astype(jnp.bfloat16), "head", scatter_dimension=1, tiled=True
    ).astype(jnp.float32)
    squares = lax.psum(jnp.sum(share * share, axis=1), "head")
    return (share * lax.rsqrt(squares[:, None] / full_width + epsilon)).astype(jnp.bfloat16)


def in_vmem(*arrays):
    return [pltpu.with_memory_space_constraint(array, pltpu.VMEM) for array in arrays]


def in_hbm(*arrays):
    return [pltpu.with_memory_space_constraint(array, pltpu.HBM) for array in arrays]


def normed(values, gain):
    mean_square = jnp.mean(values * values, axis=1, keepdims=True)
    return (values * lax.rsqrt(mean_square + epsilon) * gain).astype(jnp.bfloat16)


def pick_rows(positions, first, cells):
    picks, rows = positions.shape[0], cells.shape[0]
    row = lax.broadcasted_iota(jnp.int32, (picks, rows), 0)
    column = lax.broadcasted_iota(jnp.int32, (picks, rows), 1)
    chosen = jnp.zeros((picks, rows), jnp.int32)
    for pick in range(picks):
        chosen = jnp.where(row == pick, positions[pick] - first, chosen)
    one_hot = jnp.where(chosen == column, 1.0, 0.0).astype(jnp.bfloat16)
    return jnp.dot(one_hot, cells, preferred_element_type=jnp.float32)


def fetch(sources, targets, semaphores):
    copies = [
        pltpu.make_async_copy(source, target, semaphores.at[number])
        for number, (source, target) in enumerate(zip(sources, targets))
    ]
    for copy in copies:
        copy.start()
    return copies


def anchor_kernel(*refs):
    sources, anchors, targets, semaphores = refs[:6], refs[6], refs[7:13], refs[13]
    vol_position, surf_position, vol, surf, vol_gain, surf_gain = targets
    for copy in fetch(sources, targets, semaphores):
        copy.wait()
    block_index = lax.axis_index("tok")
    vol_rows = pick_rows(vol_position, block_index * vol.shape[0], vol[...])
    surf_rows = pick_rows(surf_position, block_index * surf.shape[0], surf[...])
    parts = [normed(vol_rows, vol_gain[...]), normed(surf_rows, surf_gain[...])]
    stacked = jnp.concatenate([part.astype(jnp.float32) for part in parts], axis=0)
    anchors[...] = stacked.astype(jnp.bfloat16)


def query_kernel(*refs):
    sources, (queries, lookup, value_turned, final) = refs[:6], refs[6:10]
    (vol, gain, projection, value_projection), semaphores = refs[10:14], refs[14]
    targets = (vol, gain, projection, value_projection, lookup, final)
    copies = fetch(sources, targets, semaphores)
    for copy in copies[:3]:
        copy.wait()
    vol_normed = normed(vol[...].astype(jnp.float32), gain[...])
    cells = vol.shape[0]
    columns = lax.dot_general(
        projection[...], vol_normed, (((0,), (1,)), ((), ())), preferred_element_type=jnp.float32
    ).astype(jnp.bfloat16)
    pairs, pair_width, _ = queries.shape
    half = pair_width // 2
    upper = lax.broadcasted_iota(jnp.int32, (pair_width, cells), 0) < half
    for pair in range(pairs):
        block = columns[pair * pair_width : (pair + 1) * pair_width, :].astype(jnp.float32)
        queries[pair, :, :cells] = jnp.where(upper, block, 0.0).astype(jnp.bfloat16)
        queries[pair, :, cells:] = jnp.where(upper, 0.0, block).astype(jnp.bfloat16)
    copies[3].wait()
    value_turned[...] = value_projection[...].T
    for copy in copies[4:]:
        copy.wait()


def attention_kernel(block_count, divisor, queries, lookup, value_turned, final, *rest):
    blocks, terms, context = rest[:block_count], rest[block_count], rest[block_count + 1]
    pairs, pair_width, wide = queries.shape
    half, cells = pair_width // 2, wide // 2
    rows = [block[...].astype(jnp.float32) for block in blocks[:-2]]
    first_core = lax.axis_index("head") == 0
    rows.append(
        jnp.where(
            first_core, blocks[-2][...].astype(jnp.float32), blocks[-1][...].astype(jnp.float32)
        )
    )
    anchors = jnp.concatenate(rows, axis=0).astype(jnp.bfloat16)
    keys = jnp.dot(anchors, lookup[...], preferred_element_type=jnp.float32).astype(jnp.bfloat16)
    values = lax.dot_general(
        value_turned[...], anchors, (((1,), (1,)), ((), ())), preferred_element_type=jnp.float32
    ).astype(jnp.bfloat16)
    left = lax.broadcasted_iota(jnp.int32, (1, wide), 1) < cells
    scale = 1.0 / math.sqrt(half)
    for pair in range(pairs):
        span = slice(pair * pair_width, (pair + 1) * pair_width)
        multiplier = jnp.where(left, divisor[2 * pair] * scale, divisor[2 * pair + 1] * scale)
        scores = jnp.dot(keys[:, span], queries[pair], preferred_element_type=jnp.float32) * multiplier
        exp_scores = jnp.exp(scores - jnp.max(scores, axis=0, keepdims=True))
        denominator = jnp.sum(exp_scores, axis=0, keepdims=True)
        added = jnp.dot(
            values[span, :], exp_scores.astype(jnp.bfloat16), preferred_element_type=jnp.float32
        )
        added = added / denominator
        context[span, :] = jnp.concatenate(
            [added[:half, :cells], added[half:, cells:]], axis=0
        ).astype(jnp.bfloat16)
    terms[...] = lax.dot_general(
        context[...], final[...], (((0,), (0,)), ((), ())), preferred_element_type=jnp.float32
    ).astype(jnp.bfloat16)


def finish_kernel(own, other, update):
    mixed = own[...].astype(jnp.float32) + other[...].astype(jnp.float32)
    factor = lax.rsqrt(jnp.mean(mixed * mixed, axis=1, keepdims=True) + epsilon)
    width = update.shape[1]
    for part in range(mixed.shape[1] // width):

        @pl.when(lax.axis_index("head") == part)
        def _():
            update[...] = (mixed[:, part * width : (part + 1) * width] * factor).astype(update.dtype)


SMEM = pl.BlockSpec(memory_space=pltpu.SMEM)
VMEM = pl.BlockSpec(memory_space=pltpu.VMEM)
HBM = pl.BlockSpec(memory_space=pltpu.HBM)
PARAMS = pltpu.CompilerParams(vmem_limit_bytes=32 * 1024 * 1024)


def direct_body(
    shards,
    interior_element_embedding,
    boundary_element_embedding,
    interior_landmark_position,
    boundary_landmark_position,
    interior_rescaling_factor,
    boundary_rescaling_factor,
    question_projection_matrix,
    lookup_projection_matrix,
    content_projection_matrix,
    final_projection_matrix,
    channel_logit_divisor,
):
    cells, width = interior_element_embedding.shape
    local_width = question_projection_matrix.shape[1]
    heads = channel_logit_divisor.shape[0]
    pair_width = 2 * (local_width // heads)
    picks = interior_landmark_position.shape[0] + boundary_landmark_position.shape[0]
    vol_gain = interior_rescaling_factor.reshape(1, width)
    surf_gain = boundary_rescaling_factor.reshape(1, width)
    anchors = pl.pallas_call(
        anchor_kernel,
        out_shape=jax.ShapeDtypeStruct((picks, width), jnp.bfloat16),
        in_specs=[HBM] * 6,
        out_specs=VMEM,
        scratch_shapes=[
            pltpu.SMEM(interior_landmark_position.shape, jnp.int32),
            pltpu.SMEM(boundary_landmark_position.shape, jnp.int32),
            pltpu.VMEM(interior_element_embedding.shape, jnp.bfloat16),
            pltpu.VMEM(boundary_element_embedding.shape, jnp.bfloat16),
            pltpu.VMEM((1, width), jnp.float32),
            pltpu.VMEM((1, width), jnp.float32),
            pltpu.SemaphoreType.DMA((6,)),
        ],
        compiler_params=PARAMS,
        name="anchors",
    )(
        *in_hbm(
            interior_landmark_position,
            boundary_landmark_position,
            interior_element_embedding,
            boundary_element_embedding,
            vol_gain,
            surf_gain,
        )
    )
    evens = list(range(2, shards, 2))
    order = [evens.pop(0 if turn % 2 == 0 else -1) for turn in range(len(evens))] + [shards - 1]
    rounds = list(zip(order, [*range(1, shards - 1, 2), 0]))
    arrived = [
        lax.ppermute(
            anchors,
            ("tok", "head"),
            [(2 * t + core, 2 * ((t + hop[core]) % shards) + core) for t in range(shards) for core in (0, 1)],
        )
        for hop in rounds[::-1]
    ]
    queries, *weights = pl.pallas_call(
        query_kernel,
        out_shape=(
            jax.ShapeDtypeStruct((heads // 2, pair_width, 2 * cells), jnp.bfloat16),
            jax.ShapeDtypeStruct((width, local_width), jnp.bfloat16),
            jax.ShapeDtypeStruct((local_width, width), jnp.bfloat16),
            jax.ShapeDtypeStruct((local_width, width), jnp.bfloat16),
        ),
        in_specs=[HBM] * 6,
        out_specs=(VMEM,) * 4,
        scratch_shapes=[
            pltpu.VMEM((cells, width), jnp.bfloat16),
            pltpu.VMEM((1, width), jnp.float32),
            pltpu.VMEM((width, local_width), jnp.bfloat16),
            pltpu.VMEM((width, local_width), jnp.bfloat16),
            pltpu.SemaphoreType.DMA((6,)),
        ],
        compiler_params=PARAMS,
        cost_estimate=pl.CostEstimate(
            flops=2 * cells * width * local_width, bytes_accessed=8 * width * local_width, transcendentals=0
        ),
        name="queries",
    )(
        *in_hbm(
            interior_element_embedding,
            vol_gain,
            question_projection_matrix,
            content_projection_matrix,
            lookup_projection_matrix,
            final_projection_matrix,
        )
    )
    *arrived, queries = lax.optimization_barrier((*arrived, queries))
    swapped = [lax.ppermute(block, "head", [(0, 1), (1, 0)]) for block in arrived]
    blocks = [anchors, *arrived[1:], *swapped[1:], arrived[0], swapped[0]]
    terms = pl.pallas_call(
        functools.partial(attention_kernel, len(blocks)),
        out_shape=jax.ShapeDtypeStruct((cells, width), jnp.bfloat16),
        in_specs=[SMEM] + [VMEM] * (4 + len(blocks)),
        out_specs=VMEM,
        scratch_shapes=[pltpu.VMEM((local_width, cells), jnp.bfloat16)],
        compiler_params=PARAMS,
        name="attention",
    )(
        channel_logit_divisor,
        *in_vmem(queries, *weights, *blocks),
    )
    other = lax.ppermute(terms, "head", [(0, 1), (1, 0)])
    return pl.pallas_call(
        finish_kernel,
        out_shape=jax.ShapeDtypeStruct((cells, local_width), jnp.bfloat16),
        in_specs=[VMEM, VMEM],
        out_specs=VMEM,
        compiler_params=PARAMS,
        name="finish",
    )(*in_vmem(terms, other))


def solution(mesh):
    placed = (
        P(("groups", "tok"), None),
        P(("groups", "tok"), None),
        P(("groups", "tok")),
        P(("groups", "tok")),
        P(),
        P(),
        P(None, "head"),
        P(None, "head"),
        P(None, "head"),
        P("head", None),
        P("head"),
    )
    shards = mesh.shape["tok"]
    small = shards % 2 == 0 and shards <= 16 and mesh.shape["head"] == 2
    body = functools.partial(direct_body, shards) if small else gathered_body
    return jax.shard_map(
        body, mesh=mesh, in_specs=placed, out_specs=P(("groups", "tok"), "head"), check_vma=False
    )
```

```python
import functools
import math

import jax
import jax.numpy as jnp
from jax import lax
from jax.experimental import pallas as pl
from jax.experimental.pallas import tpu as pltpu
from jax.sharding import PartitionSpec as P

epsilon = 1e-06
key_block = 512


def rms_rows(cells, gain):
    values = cells.astype(jnp.float32)
    mean_square = jnp.mean(values * values, axis=1, keepdims=True)
    return (values * lax.rsqrt(mean_square + epsilon) * gain).astype(jnp.bfloat16)


def absorb(running, key_rows, value_rows, queries, logit_multiplier):
    run_max, denominator, accumulated = running
    parallel_channel_total, channel_dimension, cell_count = queries.shape
    key_heads = key_rows.reshape(key_rows.shape[0], parallel_channel_total, channel_dimension)
    value_heads = value_rows.reshape(value_rows.shape[0], parallel_channel_total, channel_dimension)
    scores = (
        jnp.einsum("jhd,hdc->hjc", key_heads, queries, preferred_element_type=jnp.float32)
        * logit_multiplier
    )
    new_max = jnp.maximum(run_max, jnp.max(scores, axis=1))
    shrink = jnp.exp(run_max - new_max)
    exp_scores = jnp.exp(scores - new_max[:, None, :])
    denominator = denominator * shrink + jnp.sum(exp_scores, axis=1)
    added = jnp.einsum(
        "jhd,hjc->hdc",
        value_heads,
        exp_scores.astype(jnp.bfloat16),
        preferred_element_type=jnp.float32,
    )
    accumulated = accumulated * shrink[:, None, :] + added
    return (new_max, denominator, accumulated)


def make_folder(queries, logit_multiplier):

    def folder(running, shard_rows, offset):
        key_rows, value_rows = shard_rows
        row_count = key_rows.shape[0]
        if row_count > key_block and row_count % key_block == 0:
            row_width = key_rows.shape[1]

            def scan_step(state, key_pair):
                return (absorb(state, key_pair[0], key_pair[1], queries, logit_multiplier), None)

            stacked = (
                key_rows.reshape(row_count // key_block, key_block, row_width),
                value_rows.reshape(row_count // key_block, key_block, row_width),
            )
            running, unused = lax.scan(scan_step, running, stacked)
            return running
        return absorb(running, key_rows, value_rows, queries, logit_multiplier)

    return folder


def project_pair(rows_in, lookup_projection_matrix, content_projection_matrix):
    key_rows = jnp.dot(
        rows_in, lookup_projection_matrix, preferred_element_type=jnp.float32
    ).astype(jnp.bfloat16)
    value_rows = jnp.dot(
        rows_in, content_projection_matrix, preferred_element_type=jnp.float32
    ).astype(jnp.bfloat16)
    return (key_rows, value_rows)


def gathered_body(
    interior_element_embedding,
    boundary_element_embedding,
    interior_landmark_position,
    boundary_landmark_position,
    interior_rescaling_factor,
    boundary_rescaling_factor,
    question_projection_matrix,
    lookup_projection_matrix,
    content_projection_matrix,
    final_projection_matrix,
    channel_logit_divisor,
):
    block_index = lax.axis_index("tok")
    vol_normed = rms_rows(interior_element_embedding, interior_rescaling_factor)
    vol_local = interior_landmark_position - block_index * interior_element_embedding.shape[0]
    surf_local = boundary_landmark_position - block_index * boundary_element_embedding.shape[0]
    vol_picked = jnp.take(vol_normed, vol_local, axis=0)
    surf_picked = rms_rows(
        jnp.take(boundary_element_embedding, surf_local, axis=0), boundary_rescaling_factor
    )
    parallel_channel_total = channel_logit_divisor.shape[0]
    local_width = question_projection_matrix.shape[1]
    channel_dimension = local_width // parallel_channel_total
    cell_count = interior_element_embedding.shape[0]
    query_cols = lax.dot_general(
        question_projection_matrix,
        vol_normed,
        (((0,), (1,)), ((), ())),
        preferred_element_type=jnp.float32,
    )
    queries = query_cols.astype(jnp.bfloat16).reshape(
        parallel_channel_total, channel_dimension, cell_count
    )
    logit_multiplier = (channel_logit_divisor * (1.0 / math.sqrt(channel_dimension)))[:, None, None]
    start_state = (
        jnp.full((parallel_channel_total, cell_count), -1e30, jnp.float32),
        jnp.zeros((parallel_channel_total, cell_count), jnp.float32),
        jnp.zeros((parallel_channel_total, channel_dimension, cell_count), jnp.float32),
    )
    folder = make_folder(queries, logit_multiplier)
    anchors = jnp.concatenate([vol_picked, surf_picked], axis=0)
    anchor_keys, anchor_values = project_pair(
        anchors, lookup_projection_matrix, content_projection_matrix
    )
    final_state = folder(
        start_state,
        (
            lax.all_gather(anchor_keys, "tok", axis=0, tiled=True),
            lax.all_gather(anchor_values, "tok", axis=0, tiled=True),
        ),
        jnp.int32(0),
    )
    run_max, denominator, accumulated = final_state
    context = (
        (accumulated / denominator[:, None, :])
        .astype(jnp.bfloat16)
        .reshape(local_width, cell_count)
    )
    head_terms = lax.dot_general(
        context,
        final_projection_matrix,
        (((0,), (0,)), ((), ())),
        preferred_element_type=jnp.float32,
    )
    full_width = head_terms.shape[1]
    share = lax.psum_scatter(
        head_terms.astype(jnp.bfloat16), "head", scatter_dimension=1, tiled=True
    ).astype(jnp.float32)
    squares = lax.psum(jnp.sum(share * share, axis=1), "head")
    return (share * lax.rsqrt(squares[:, None] / full_width + epsilon)).astype(jnp.bfloat16)


def in_vmem(*arrays):
    return [pltpu.with_memory_space_constraint(array, pltpu.VMEM) for array in arrays]


def in_hbm(*arrays):
    return [pltpu.with_memory_space_constraint(array, pltpu.HBM) for array in arrays]


def normed(values, gain):
    mean_square = jnp.mean(values * values, axis=1, keepdims=True)
    return (values * lax.rsqrt(mean_square + epsilon) * gain).astype(jnp.bfloat16)


def pick_rows(positions, first, cells):
    picks, rows = positions.shape[0], cells.shape[0]
    row = lax.broadcasted_iota(jnp.int32, (picks, rows), 0)
    column = lax.broadcasted_iota(jnp.int32, (picks, rows), 1)
    chosen = jnp.zeros((picks, rows), jnp.int32)
    for pick in range(picks):
        chosen = jnp.where(row == pick, positions[pick] - first, chosen)
    one_hot = jnp.where(chosen == column, 1.0, 0.0).astype(jnp.bfloat16)
    return jnp.dot(one_hot, cells, preferred_element_type=jnp.float32)


def fetch(sources, targets, semaphores):
    copies = [
        pltpu.make_async_copy(source, target, semaphores.at[number])
        for number, (source, target) in enumerate(zip(sources, targets))
    ]
    for copy in copies:
        copy.start()
    return copies


def anchor_kernel(*refs):
    sources, anchors, targets, semaphores = refs[:6], refs[6], refs[7:13], refs[13]
    vol_position, surf_position, vol, surf, vol_gain, surf_gain = targets
    for copy in fetch(sources, targets, semaphores):
        copy.wait()
    block_index = lax.axis_index("tok")
    vol_rows = pick_rows(vol_position, block_index * vol.shape[0], vol[...])
    surf_rows = pick_rows(surf_position, block_index * surf.shape[0], surf[...])
    parts = [normed(vol_rows, vol_gain[...]), normed(surf_rows, surf_gain[...])]
    stacked = jnp.concatenate([part.astype(jnp.float32) for part in parts], axis=0)
    anchors[...] = stacked.astype(jnp.bfloat16)


def query_kernel(*refs):
    sources, (queries, multiplier, lookup, value_turned, final) = refs[:7], refs[7:12]
    (vol, gain, projection, divisor, value_projection), semaphores = refs[12:17], refs[17]
    targets = (vol, gain, projection, divisor, value_projection, lookup, final)
    copies = fetch(sources, targets, semaphores)
    for copy in copies[:4]:
        copy.wait()
    vol_normed = normed(vol[...].astype(jnp.float32), gain[...])
    cells = vol.shape[0]
    columns = lax.dot_general(
        projection[...], vol_normed, (((0,), (1,)), ((), ())), preferred_element_type=jnp.float32
    ).astype(jnp.bfloat16)
    pairs, pair_width, _ = queries.shape
    half = pair_width // 2
    left = lax.broadcasted_iota(jnp.int32, (1, 2 * cells), 1) < cells
    scale = 1.0 / math.sqrt(half)
    for pair in range(pairs):
        multiplier[pair : pair + 1, :] = jnp.where(
            left, divisor[2 * pair] * scale, divisor[2 * pair + 1] * scale
        )
    upper = lax.broadcasted_iota(jnp.int32, (pair_width, cells), 0) < half
    for pair in range(pairs):
        block = columns[pair * pair_width : (pair + 1) * pair_width, :].astype(jnp.float32)
        queries[pair, :, :cells] = jnp.where(upper, block, 0.0).astype(jnp.bfloat16)
        queries[pair, :, cells:] = jnp.where(upper, 0.0, block).astype(jnp.bfloat16)
    copies[4].wait()
    value_turned[...] = value_projection[...].T
    for copy in copies[5:]:
        copy.wait()


def attention_kernel(block_count, queries, multiplier, lookup, value_turned, final, *rest):
    blocks, terms, context = rest[:block_count], rest[block_count], rest[block_count + 1]
    pairs, pair_width, wide = queries.shape
    half, cells = pair_width // 2, wide // 2
    rows = [block[...].astype(jnp.float32) for block in blocks]
    anchors = jnp.concatenate(rows, axis=0).astype(jnp.bfloat16)
    keys = jnp.dot(anchors, lookup[...], preferred_element_type=jnp.float32).astype(jnp.bfloat16)
    values = lax.dot_general(
        value_turned[...], anchors, (((1,), (1,)), ((), ())), preferred_element_type=jnp.float32
    ).astype(jnp.bfloat16)
    for pair in range(pairs):
        span = slice(pair * pair_width, (pair + 1) * pair_width)
        scores = jnp.dot(keys[:, span], queries[pair], preferred_element_type=jnp.float32)
        scores = scores * multiplier[pair : pair + 1, :]
        exp_scores = jnp.exp(scores - jnp.max(scores, axis=0, keepdims=True))
        denominator = jnp.sum(exp_scores, axis=0, keepdims=True)
        added = jnp.dot(
            values[span, :], exp_scores.astype(jnp.bfloat16), preferred_element_type=jnp.float32
        )
        added = added / denominator
        context[span, :] = jnp.concatenate(
            [added[:half, :cells], added[half:, cells:]], axis=0
        ).astype(jnp.bfloat16)
    terms[...] = lax.dot_general(
        context[...], final[...], (((0,), (0,)), ((), ())), preferred_element_type=jnp.float32
    ).astype(jnp.bfloat16)


def finish_kernel(own, other, update):
    mixed = own[...].astype(jnp.float32) + other[...].astype(jnp.float32)
    factor = lax.rsqrt(jnp.mean(mixed * mixed, axis=1, keepdims=True) + epsilon)
    width = update.shape[1]
    for part in range(mixed.shape[1] // width):

        @pl.when(lax.axis_index("head") == part)
        def _():
            update[...] = (mixed[:, part * width : (part + 1) * width] * factor).astype(update.dtype)


VMEM = pl.BlockSpec(memory_space=pltpu.VMEM)
HBM = pl.BlockSpec(memory_space=pltpu.HBM)
PARAMS = pltpu.CompilerParams(vmem_limit_bytes=32 * 1024 * 1024)


def direct_body(
    shards,
    interior_element_embedding,
    boundary_element_embedding,
    interior_landmark_position,
    boundary_landmark_position,
    interior_rescaling_factor,
    boundary_rescaling_factor,
    question_projection_matrix,
    lookup_projection_matrix,
    content_projection_matrix,
    final_projection_matrix,
    channel_logit_divisor,
):
    cells, width = interior_element_embedding.shape
    local_width = question_projection_matrix.shape[1]
    heads = channel_logit_divisor.shape[0]
    pair_width = 2 * (local_width // heads)
    picks = interior_landmark_position.shape[0] + boundary_landmark_position.shape[0]
    vol_gain = interior_rescaling_factor.reshape(1, width)
    surf_gain = boundary_rescaling_factor.reshape(1, width)
    anchors = pl.pallas_call(
        anchor_kernel,
        out_shape=jax.ShapeDtypeStruct((picks, width), jnp.bfloat16),
        in_specs=[HBM] * 6,
        out_specs=VMEM,
        scratch_shapes=[
            pltpu.SMEM(interior_landmark_position.shape, jnp.int32),
            pltpu.SMEM(boundary_landmark_position.shape, jnp.int32),
            pltpu.VMEM(interior_element_embedding.shape, jnp.bfloat16),
            pltpu.VMEM(boundary_element_embedding.shape, jnp.bfloat16),
            pltpu.VMEM((1, width), jnp.float32),
            pltpu.VMEM((1, width), jnp.float32),
            pltpu.SemaphoreType.DMA((6,)),
        ],
        compiler_params=PARAMS,
        name="anchors",
    )(
        *in_hbm(
            interior_landmark_position,
            boundary_landmark_position,
            interior_element_embedding,
            boundary_element_embedding,
            vol_gain,
            surf_gain,
        )
    )
    rounds = [(hop + 1, hop) for hop in range(1, shards - 1, 2)] + [(shards - 1, shards - 1)]
    arrived = [
        lax.ppermute(
            anchors,
            ("tok", "head"),
            [(2 * t + core, 2 * ((t + hop[core]) % shards) + core) for t in range(shards) for core in (0, 1)],
        )
        for hop in rounds[::-1]
    ]
    queries, *weights = pl.pallas_call(
        query_kernel,
        out_shape=(
            jax.ShapeDtypeStruct((heads // 2, pair_width, 2 * cells), jnp.bfloat16),
            jax.ShapeDtypeStruct((heads // 2, 2 * cells), jnp.float32),
            jax.ShapeDtypeStruct((width, local_width), jnp.bfloat16),
            jax.ShapeDtypeStruct((local_width, width), jnp.bfloat16),
            jax.ShapeDtypeStruct((local_width, width), jnp.bfloat16),
        ),
        in_specs=[HBM] * 7,
        out_specs=(VMEM,) * 5,
        scratch_shapes=[
            pltpu.VMEM((cells, width), jnp.bfloat16),
            pltpu.VMEM((1, width), jnp.float32),
            pltpu.VMEM((width, local_width), jnp.bfloat16),
            pltpu.SMEM((heads,), jnp.float32),
            pltpu.VMEM((width, local_width), jnp.bfloat16),
            pltpu.SemaphoreType.DMA((7,)),
        ],
        compiler_params=PARAMS,
        cost_estimate=pl.CostEstimate(
            flops=2 * cells * width * local_width, bytes_accessed=8 * width * local_width, transcendentals=0
        ),
        name="queries",
    )(
        *in_hbm(
            interior_element_embedding,
            vol_gain,
            question_projection_matrix,
            channel_logit_divisor,
            content_projection_matrix,
            lookup_projection_matrix,
            final_projection_matrix,
        )
    )
    swapped = [lax.ppermute(block, "head", [(0, 1), (1, 0)]) for block in arrived[1:]]
    blocks = [anchors, *arrived, *swapped]
    terms = pl.pallas_call(
        functools.partial(attention_kernel, len(blocks)),
        out_shape=jax.ShapeDtypeStruct((cells, width), jnp.bfloat16),
        in_specs=[VMEM] * (5 + len(blocks)),
        out_specs=VMEM,
        scratch_shapes=[pltpu.VMEM((local_width, cells), jnp.bfloat16)],
        compiler_params=PARAMS,
        name="attention",
    )(
        *in_vmem(queries, *weights, *blocks),
    )
    other = lax.ppermute(terms, "head", [(0, 1), (1, 0)])
    return pl.pallas_call(
        finish_kernel,
        out_shape=jax.ShapeDtypeStruct((cells, local_width), jnp.bfloat16),
        in_specs=[VMEM, VMEM],
        out_specs=VMEM,
        compiler_params=PARAMS,
        name="finish",
    )(*in_vmem(terms, other))


def solution(mesh):
    placed = (
        P(("groups", "tok"), None),
        P(("groups", "tok"), None),
        P(("groups", "tok")),
        P(("groups", "tok")),
        P(),
        P(),
        P(None, "head"),
        P(None, "head"),
        P(None, "head"),
        P("head", None),
        P("head"),
    )
    shards = mesh.shape["tok"]
    small = shards % 2 == 0 and shards <= 16 and mesh.shape["head"] == 2
    body = functools.partial(direct_body, shards) if small else gathered_body
    return jax.shard_map(
        body, mesh=mesh, in_specs=placed, out_specs=P(("groups", "tok"), "head"), check_vma=False
    )
```

```python
import functools
import math

import jax
import jax.numpy as jnp
from jax import lax
from jax.experimental import pallas as pl
from jax.experimental.pallas import tpu as pltpu
from jax.sharding import PartitionSpec as P

epsilon = 1e-06
key_block = 512


def rms_rows(cells, gain):
    values = cells.astype(jnp.float32)
    mean_square = jnp.mean(values * values, axis=1, keepdims=True)
    return (values * lax.rsqrt(mean_square + epsilon) * gain).astype(jnp.bfloat16)


def absorb(running, key_rows, value_rows, queries, logit_multiplier):
    run_max, denominator, accumulated = running
    parallel_channel_total, channel_dimension, cell_count = queries.shape
    key_heads = key_rows.reshape(key_rows.shape[0], parallel_channel_total, channel_dimension)
    value_heads = value_rows.reshape(value_rows.shape[0], parallel_channel_total, channel_dimension)
    scores = (
        jnp.einsum("jhd,hdc->hjc", key_heads, queries, preferred_element_type=jnp.float32)
        * logit_multiplier
    )
    new_max = jnp.maximum(run_max, jnp.max(scores, axis=1))
    shrink = jnp.exp(run_max - new_max)
    exp_scores = jnp.exp(scores - new_max[:, None, :])
    denominator = denominator * shrink + jnp.sum(exp_scores, axis=1)
    added = jnp.einsum(
        "jhd,hjc->hdc",
        value_heads,
        exp_scores.astype(jnp.bfloat16),
        preferred_element_type=jnp.float32,
    )
    accumulated = accumulated * shrink[:, None, :] + added
    return (new_max, denominator, accumulated)


def make_folder(queries, logit_multiplier):

    def folder(running, shard_rows, offset):
        key_rows, value_rows = shard_rows
        row_count = key_rows.shape[0]
        if row_count > key_block and row_count % key_block == 0:
            row_width = key_rows.shape[1]

            def scan_step(state, key_pair):
                return (absorb(state, key_pair[0], key_pair[1], queries, logit_multiplier), None)

            stacked = (
                key_rows.reshape(row_count // key_block, key_block, row_width),
                value_rows.reshape(row_count // key_block, key_block, row_width),
            )
            running, unused = lax.scan(scan_step, running, stacked)
            return running
        return absorb(running, key_rows, value_rows, queries, logit_multiplier)

    return folder


def project_pair(rows_in, lookup_projection_matrix, content_projection_matrix):
    key_rows = jnp.dot(
        rows_in, lookup_projection_matrix, preferred_element_type=jnp.float32
    ).astype(jnp.bfloat16)
    value_rows = jnp.dot(
        rows_in, content_projection_matrix, preferred_element_type=jnp.float32
    ).astype(jnp.bfloat16)
    return (key_rows, value_rows)


def gathered_body(
    interior_element_embedding,
    boundary_element_embedding,
    interior_landmark_position,
    boundary_landmark_position,
    interior_rescaling_factor,
    boundary_rescaling_factor,
    question_projection_matrix,
    lookup_projection_matrix,
    content_projection_matrix,
    final_projection_matrix,
    channel_logit_divisor,
):
    block_index = lax.axis_index("tok")
    vol_normed = rms_rows(interior_element_embedding, interior_rescaling_factor)
    vol_local = interior_landmark_position - block_index * interior_element_embedding.shape[0]
    surf_local = boundary_landmark_position - block_index * boundary_element_embedding.shape[0]
    vol_picked = jnp.take(vol_normed, vol_local, axis=0)
    surf_picked = rms_rows(
        jnp.take(boundary_element_embedding, surf_local, axis=0), boundary_rescaling_factor
    )
    parallel_channel_total = channel_logit_divisor.shape[0]
    local_width = question_projection_matrix.shape[1]
    channel_dimension = local_width // parallel_channel_total
    cell_count = interior_element_embedding.shape[0]
    query_cols = lax.dot_general(
        question_projection_matrix,
        vol_normed,
        (((0,), (1,)), ((), ())),
        preferred_element_type=jnp.float32,
    )
    queries = query_cols.astype(jnp.bfloat16).reshape(
        parallel_channel_total, channel_dimension, cell_count
    )
    logit_multiplier = (channel_logit_divisor * (1.0 / math.sqrt(channel_dimension)))[:, None, None]
    start_state = (
        jnp.full((parallel_channel_total, cell_count), -1e30, jnp.float32),
        jnp.zeros((parallel_channel_total, cell_count), jnp.float32),
        jnp.zeros((parallel_channel_total, channel_dimension, cell_count), jnp.float32),
    )
    folder = make_folder(queries, logit_multiplier)
    anchors = jnp.concatenate([vol_picked, surf_picked], axis=0)
    anchor_keys, anchor_values = project_pair(
        anchors, lookup_projection_matrix, content_projection_matrix
    )
    final_state = folder(
        start_state,
        (
            lax.all_gather(anchor_keys, "tok", axis=0, tiled=True),
            lax.all_gather(anchor_values, "tok", axis=0, tiled=True),
        ),
        jnp.int32(0),
    )
    run_max, denominator, accumulated = final_state
    context = (
        (accumulated / denominator[:, None, :])
        .astype(jnp.bfloat16)
        .reshape(local_width, cell_count)
    )
    head_terms = lax.dot_general(
        context,
        final_projection_matrix,
        (((0,), (0,)), ((), ())),
        preferred_element_type=jnp.float32,
    )
    full_width = head_terms.shape[1]
    share = lax.psum_scatter(
        head_terms.astype(jnp.bfloat16), "head", scatter_dimension=1, tiled=True
    ).astype(jnp.float32)
    squares = lax.psum(jnp.sum(share * share, axis=1), "head")
    return (share * lax.rsqrt(squares[:, None] / full_width + epsilon)).astype(jnp.bfloat16)


def in_vmem(*arrays):
    return [pltpu.with_memory_space_constraint(array, pltpu.VMEM) for array in arrays]


def in_hbm(*arrays):
    return [pltpu.with_memory_space_constraint(array, pltpu.HBM) for array in arrays]


def normed(values, gain):
    mean_square = jnp.mean(values * values, axis=1, keepdims=True)
    return (values * lax.rsqrt(mean_square + epsilon) * gain).astype(jnp.bfloat16)


def pick_rows(positions, first, cells):
    picks, rows = positions.shape[0], cells.shape[0]
    row = lax.broadcasted_iota(jnp.int32, (picks, rows), 0)
    column = lax.broadcasted_iota(jnp.int32, (picks, rows), 1)
    chosen = jnp.zeros((picks, rows), jnp.int32)
    for pick in range(picks):
        chosen = jnp.where(row == pick, positions[pick] - first, chosen)
    one_hot = jnp.where(chosen == column, 1.0, 0.0).astype(jnp.bfloat16)
    return jnp.dot(one_hot, cells, preferred_element_type=jnp.float32)


def fetch(sources, targets, semaphores):
    copies = [
        pltpu.make_async_copy(source, target, semaphores.at[number])
        for number, (source, target) in enumerate(zip(sources, targets))
    ]
    for copy in copies:
        copy.start()
    return copies


def anchor_kernel(*refs):
    sources, (anchors, vol, vol_gain, multiplier), rest = refs[:7], refs[7:11], refs[11:]
    vol_position, surf_position, surf, surf_gain, divisor, semaphores = rest
    targets = (vol_position, surf_position, vol, surf, vol_gain, surf_gain, divisor)
    for copy in fetch(sources, targets, semaphores):
        copy.wait()
    block_index = lax.axis_index("tok")
    vol_rows = pick_rows(vol_position, block_index * vol.shape[0], vol[...])
    surf_rows = pick_rows(surf_position, block_index * surf.shape[0], surf[...])
    parts = [normed(vol_rows, vol_gain[...]), normed(surf_rows, surf_gain[...])]
    stacked = jnp.concatenate([part.astype(jnp.float32) for part in parts], axis=0)
    anchors[...] = stacked.astype(jnp.bfloat16)
    pairs, wide = multiplier.shape
    left = lax.broadcasted_iota(jnp.int32, (1, wide), 1) < wide // 2
    for pair in range(pairs):
        multiplier[pair : pair + 1, :] = jnp.where(left, divisor[2 * pair], divisor[2 * pair + 1])


def query_kernel(vol, gain, projection, value_projection, lookup, final, queries, value_turned):
    vol_normed = normed(vol[...].astype(jnp.float32), gain[...])
    cells = vol.shape[0]
    columns = lax.dot_general(
        projection[...], vol_normed, (((0,), (1,)), ((), ())), preferred_element_type=jnp.float32
    ).astype(jnp.bfloat16)
    pairs, pair_width, _ = queries.shape
    upper = lax.broadcasted_iota(jnp.int32, (pair_width, cells), 0) < pair_width // 2
    for pair in range(pairs):
        block = columns[pair * pair_width : (pair + 1) * pair_width, :].astype(jnp.float32)
        queries[pair, :, :cells] = jnp.where(upper, block, 0.0).astype(jnp.bfloat16)
        queries[pair, :, cells:] = jnp.where(upper, 0.0, block).astype(jnp.bfloat16)
    value_turned[...] = value_projection[...].T


def attention_kernel(block_count, queries, multiplier, lookup, value_turned, final, *rest):
    blocks, terms, context = rest[:block_count], rest[block_count], rest[block_count + 1]
    pairs, pair_width, wide = queries.shape
    half, cells = pair_width // 2, wide // 2
    rows = [block[...].astype(jnp.float32) for block in blocks]
    anchors = jnp.concatenate(rows, axis=0).astype(jnp.bfloat16)
    keys = jnp.dot(anchors, lookup[...], preferred_element_type=jnp.float32).astype(jnp.bfloat16)
    values = lax.dot_general(
        value_turned[...], anchors, (((1,), (1,)), ((), ())), preferred_element_type=jnp.float32
    ).astype(jnp.bfloat16)
    scale = 1.0 / math.sqrt(half)
    for pair in range(pairs):
        span = slice(pair * pair_width, (pair + 1) * pair_width)
        scores = jnp.dot(keys[:, span], queries[pair], preferred_element_type=jnp.float32)
        scores = scores * (multiplier[pair : pair + 1, :] * scale)
        exp_scores = jnp.exp(scores - jnp.max(scores, axis=0, keepdims=True))
        denominator = jnp.sum(exp_scores, axis=0, keepdims=True)
        added = jnp.dot(
            values[span, :], exp_scores.astype(jnp.bfloat16), preferred_element_type=jnp.float32
        )
        added = added / denominator
        context[span, :] = jnp.concatenate(
            [added[:half, :cells], added[half:, cells:]], axis=0
        ).astype(jnp.bfloat16)
    terms[...] = lax.dot_general(
        context[...], final[...], (((0,), (0,)), ((), ())), preferred_element_type=jnp.float32
    ).astype(jnp.bfloat16)


def finish_kernel(own, other, update):
    mixed = own[...].astype(jnp.float32) + other[...].astype(jnp.float32)
    factor = lax.rsqrt(jnp.mean(mixed * mixed, axis=1, keepdims=True) + epsilon)
    width = update.shape[1]
    for part in range(mixed.shape[1] // width):

        @pl.when(lax.axis_index("head") == part)
        def _():
            update[...] = (mixed[:, part * width : (part + 1) * width] * factor).astype(update.dtype)


VMEM = pl.BlockSpec(memory_space=pltpu.VMEM)
HBM = pl.BlockSpec(memory_space=pltpu.HBM)
PARAMS = pltpu.CompilerParams(vmem_limit_bytes=32 * 1024 * 1024)


def direct_body(
    shards,
    interior_element_embedding,
    boundary_element_embedding,
    interior_landmark_position,
    boundary_landmark_position,
    interior_rescaling_factor,
    boundary_rescaling_factor,
    question_projection_matrix,
    lookup_projection_matrix,
    content_projection_matrix,
    final_projection_matrix,
    channel_logit_divisor,
):
    cells, width = interior_element_embedding.shape
    local_width = question_projection_matrix.shape[1]
    heads = channel_logit_divisor.shape[0]
    pair_width = 2 * (local_width // heads)
    picks = interior_landmark_position.shape[0] + boundary_landmark_position.shape[0]
    anchors, vol, vol_gain, multiplier = pl.pallas_call(
        anchor_kernel,
        out_shape=(
            jax.ShapeDtypeStruct((picks, width), jnp.bfloat16),
            jax.ShapeDtypeStruct((cells, width), jnp.bfloat16),
            jax.ShapeDtypeStruct((1, width), jnp.float32),
            jax.ShapeDtypeStruct((heads // 2, 2 * cells), jnp.float32),
        ),
        in_specs=[HBM] * 7,
        out_specs=(VMEM,) * 4,
        scratch_shapes=[
            pltpu.SMEM(interior_landmark_position.shape, jnp.int32),
            pltpu.SMEM(boundary_landmark_position.shape, jnp.int32),
            pltpu.VMEM(boundary_element_embedding.shape, jnp.bfloat16),
            pltpu.VMEM((1, width), jnp.float32),
            pltpu.SMEM((heads,), jnp.float32),
            pltpu.SemaphoreType.DMA((7,)),
        ],
        compiler_params=PARAMS,
        cost_estimate=pl.CostEstimate(flops=2*10**10, bytes_accessed=2**20, transcendentals=0),
        name="anchors",
    )(
        *in_hbm(
            interior_landmark_position,
            boundary_landmark_position,
            interior_element_embedding,
            boundary_element_embedding,
            interior_rescaling_factor.reshape(1, width),
            boundary_rescaling_factor.reshape(1, width),
            channel_logit_divisor,
        )
    )
    rounds = [(hop + 1, hop) for hop in range(1, shards - 1, 2)] + [(shards - 1, shards - 1)]
    arrived = [
        lax.ppermute(
            anchors,
            ("tok", "head"),
            [(2 * t + core, 2 * ((t + hop[core]) % shards) + core) for t in range(shards) for core in (0, 1)],
        )
        for hop in rounds[-1:] + rounds[:-1]
    ]
    queries, value_turned = pl.pallas_call(
        query_kernel,
        out_shape=(
            jax.ShapeDtypeStruct((heads // 2, pair_width, 2 * cells), jnp.bfloat16),
            jax.ShapeDtypeStruct((local_width, width), jnp.bfloat16),
        ),
        in_specs=[VMEM] * 6,
        out_specs=(VMEM, VMEM),
        compiler_params=PARAMS,
        cost_estimate=pl.CostEstimate(
            flops=2 * cells * width * local_width, bytes_accessed=8 * width * local_width, transcendentals=0
        ),
        name="queries",
    )(*in_vmem(vol, vol_gain, question_projection_matrix, content_projection_matrix, lookup_projection_matrix, final_projection_matrix))
    swapped = [lax.ppermute(block, "head", [(0, 1), (1, 0)]) for block in arrived[1:]]
    blocks = [anchors, *arrived, *swapped]
    terms = pl.pallas_call(
        functools.partial(attention_kernel, len(blocks)),
        out_shape=jax.ShapeDtypeStruct((cells, width), jnp.bfloat16),
        in_specs=[VMEM] * (5 + len(blocks)),
        out_specs=VMEM,
        scratch_shapes=[pltpu.VMEM((local_width, cells), jnp.bfloat16)],
        compiler_params=PARAMS,
        name="attention",
    )(
        *in_vmem(queries, multiplier, lookup_projection_matrix, value_turned, final_projection_matrix, *blocks),
    )
    other = lax.ppermute(terms, "head", [(0, 1), (1, 0)])
    return pl.pallas_call(
        finish_kernel,
        out_shape=jax.ShapeDtypeStruct((cells, local_width), jnp.bfloat16),
        in_specs=[VMEM, VMEM],
        out_specs=VMEM,
        compiler_params=PARAMS,
        name="finish",
    )(*in_vmem(terms, other))


def solution(mesh):
    placed = (
        P(("groups", "tok"), None),
        P(("groups", "tok"), None),
        P(("groups", "tok")),
        P(("groups", "tok")),
        P(),
        P(),
        P(None, "head"),
        P(None, "head"),
        P(None, "head"),
        P("head", None),
        P("head"),
    )
    shards = mesh.shape["tok"]
    small = shards % 2 == 0 and shards <= 16 and mesh.shape["head"] == 2
    body = functools.partial(direct_body, shards) if small else gathered_body
    return jax.shard_map(
        body, mesh=mesh, in_specs=placed, out_specs=P(("groups", "tok"), "head"), check_vma=False
    )
```

```python
import functools
import math

import jax
import jax.numpy as jnp
from jax import lax
from jax.experimental import pallas as pl
from jax.experimental.pallas import tpu as pltpu
from jax.sharding import PartitionSpec as P

epsilon = 1e-06
key_block = 512


def rms_rows(cells, gain):
    values = cells.astype(jnp.float32)
    mean_square = jnp.mean(values * values, axis=1, keepdims=True)
    return (values * lax.rsqrt(mean_square + epsilon) * gain).astype(jnp.bfloat16)


def absorb(running, key_rows, value_rows, queries, logit_multiplier):
    run_max, denominator, accumulated = running
    parallel_channel_total, channel_dimension, cell_count = queries.shape
    key_heads = key_rows.reshape(key_rows.shape[0], parallel_channel_total, channel_dimension)
    value_heads = value_rows.reshape(value_rows.shape[0], parallel_channel_total, channel_dimension)
    scores = (
        jnp.einsum("jhd,hdc->hjc", key_heads, queries, preferred_element_type=jnp.float32)
        * logit_multiplier
    )
    new_max = jnp.maximum(run_max, jnp.max(scores, axis=1))
    shrink = jnp.exp(run_max - new_max)
    exp_scores = jnp.exp(scores - new_max[:, None, :])
    denominator = denominator * shrink + jnp.sum(exp_scores, axis=1)
    added = jnp.einsum(
        "jhd,hjc->hdc",
        value_heads,
        exp_scores.astype(jnp.bfloat16),
        preferred_element_type=jnp.float32,
    )
    accumulated = accumulated * shrink[:, None, :] + added
    return (new_max, denominator, accumulated)


def make_folder(queries, logit_multiplier):

    def folder(running, shard_rows, offset):
        key_rows, value_rows = shard_rows
        row_count = key_rows.shape[0]
        if row_count > key_block and row_count % key_block == 0:
            row_width = key_rows.shape[1]

            def scan_step(state, key_pair):
                return (absorb(state, key_pair[0], key_pair[1], queries, logit_multiplier), None)

            stacked = (
                key_rows.reshape(row_count // key_block, key_block, row_width),
                value_rows.reshape(row_count // key_block, key_block, row_width),
            )
            running, unused = lax.scan(scan_step, running, stacked)
            return running
        return absorb(running, key_rows, value_rows, queries, logit_multiplier)

    return folder


def project_pair(rows_in, lookup_projection_matrix, content_projection_matrix):
    key_rows = jnp.dot(
        rows_in, lookup_projection_matrix, preferred_element_type=jnp.float32
    ).astype(jnp.bfloat16)
    value_rows = jnp.dot(
        rows_in, content_projection_matrix, preferred_element_type=jnp.float32
    ).astype(jnp.bfloat16)
    return (key_rows, value_rows)


def gathered_body(
    interior_element_embedding,
    boundary_element_embedding,
    interior_landmark_position,
    boundary_landmark_position,
    interior_rescaling_factor,
    boundary_rescaling_factor,
    question_projection_matrix,
    lookup_projection_matrix,
    content_projection_matrix,
    final_projection_matrix,
    channel_logit_divisor,
):
    block_index = lax.axis_index("tok")
    vol_normed = rms_rows(interior_element_embedding, interior_rescaling_factor)
    vol_local = interior_landmark_position - block_index * interior_element_embedding.shape[0]
    surf_local = boundary_landmark_position - block_index * boundary_element_embedding.shape[0]
    vol_picked = jnp.take(vol_normed, vol_local, axis=0)
    surf_picked = rms_rows(
        jnp.take(boundary_element_embedding, surf_local, axis=0), boundary_rescaling_factor
    )
    parallel_channel_total = channel_logit_divisor.shape[0]
    local_width = question_projection_matrix.shape[1]
    channel_dimension = local_width // parallel_channel_total
    cell_count = interior_element_embedding.shape[0]
    query_cols = lax.dot_general(
        question_projection_matrix,
        vol_normed,
        (((0,), (1,)), ((), ())),
        preferred_element_type=jnp.float32,
    )
    queries = query_cols.astype(jnp.bfloat16).reshape(
        parallel_channel_total, channel_dimension, cell_count
    )
    logit_multiplier = (channel_logit_divisor * (1.0 / math.sqrt(channel_dimension)))[:, None, None]
    start_state = (
        jnp.full((parallel_channel_total, cell_count), -1e30, jnp.float32),
        jnp.zeros((parallel_channel_total, cell_count), jnp.float32),
        jnp.zeros((parallel_channel_total, channel_dimension, cell_count), jnp.float32),
    )
    folder = make_folder(queries, logit_multiplier)
    anchors = jnp.concatenate([vol_picked, surf_picked], axis=0)
    anchor_keys, anchor_values = project_pair(
        anchors, lookup_projection_matrix, content_projection_matrix
    )
    final_state = folder(
        start_state,
        (
            lax.all_gather(anchor_keys, "tok", axis=0, tiled=True),
            lax.all_gather(anchor_values, "tok", axis=0, tiled=True),
        ),
        jnp.int32(0),
    )
    run_max, denominator, accumulated = final_state
    context = (
        (accumulated / denominator[:, None, :])
        .astype(jnp.bfloat16)
        .reshape(local_width, cell_count)
    )
    head_terms = lax.dot_general(
        context,
        final_projection_matrix,
        (((0,), (0,)), ((), ())),
        preferred_element_type=jnp.float32,
    )
    full_width = head_terms.shape[1]
    share = lax.psum_scatter(
        head_terms.astype(jnp.bfloat16), "head", scatter_dimension=1, tiled=True
    ).astype(jnp.float32)
    squares = lax.psum(jnp.sum(share * share, axis=1), "head")
    return (share * lax.rsqrt(squares[:, None] / full_width + epsilon)).astype(jnp.bfloat16)


def in_vmem(*arrays):
    return [pltpu.with_memory_space_constraint(array, pltpu.VMEM) for array in arrays]


def in_hbm(*arrays):
    return [pltpu.with_memory_space_constraint(array, pltpu.HBM) for array in arrays]


def normed(values, gain):
    mean_square = jnp.mean(values * values, axis=1, keepdims=True)
    return (values * lax.rsqrt(mean_square + epsilon) * gain).astype(jnp.bfloat16)


def pick_rows(positions, first, cells):
    picks, rows = positions.shape[0], cells.shape[0]
    row = lax.broadcasted_iota(jnp.int32, (picks, rows), 0)
    column = lax.broadcasted_iota(jnp.int32, (picks, rows), 1)
    chosen = jnp.zeros((picks, rows), jnp.int32)
    for pick in range(picks):
        chosen = jnp.where(row == pick, positions[pick] - first, chosen)
    one_hot = jnp.where(chosen == column, 1.0, 0.0).astype(jnp.bfloat16)
    return jnp.dot(one_hot, cells, preferred_element_type=jnp.float32)


def fetch(sources, targets, semaphores):
    copies = [
        pltpu.make_async_copy(source, target, semaphores.at[number])
        for number, (source, target) in enumerate(zip(sources, targets))
    ]
    for copy in copies:
        copy.start()
    return copies


def anchor_kernel(*refs):
    sources, (anchors, vol, vol_gain, multiplier), rest = refs[:7], refs[7:11], refs[11:]
    vol_position, surf_position, surf, surf_gain, divisor, semaphores = rest
    targets = (vol_position, surf_position, vol, surf, vol_gain, surf_gain, divisor)
    for copy in fetch(sources, targets, semaphores):
        copy.wait()
    block_index = lax.axis_index("tok")
    vol_rows = pick_rows(vol_position, block_index * vol.shape[0], vol[...])
    surf_rows = pick_rows(surf_position, block_index * surf.shape[0], surf[...])
    parts = [normed(vol_rows, vol_gain[...]), normed(surf_rows, surf_gain[...])]
    stacked = jnp.concatenate([part.astype(jnp.float32) for part in parts], axis=0)
    anchors[...] = stacked.astype(jnp.bfloat16)
    pairs, wide = multiplier.shape
    left = lax.broadcasted_iota(jnp.int32, (1, wide), 1) < wide // 2
    for pair in range(pairs):
        multiplier[pair : pair + 1, :] = jnp.where(left, divisor[2 * pair], divisor[2 * pair + 1])


def query_kernel(vol, gain, projection, value_projection, lookup, final, queries, value_turned):
    vol_normed = normed(vol[...].astype(jnp.float32), gain[...])
    cells = vol.shape[0]
    columns = lax.dot_general(
        projection[...], vol_normed, (((0,), (1,)), ((), ())), preferred_element_type=jnp.float32
    ).astype(jnp.bfloat16)
    pairs, pair_width, _ = queries.shape
    upper = lax.broadcasted_iota(jnp.int32, (pair_width, cells), 0) < pair_width // 2
    for pair in range(pairs):
        block = columns[pair * pair_width : (pair + 1) * pair_width, :].astype(jnp.float32)
        queries[pair, :, :cells] = jnp.where(upper, block, 0.0).astype(jnp.bfloat16)
        queries[pair, :, cells:] = jnp.where(upper, 0.0, block).astype(jnp.bfloat16)
    value_turned[...] = value_projection[...].T


def attention_kernel(block_count, queries, multiplier, lookup, value_turned, final, *rest):
    blocks, terms = rest[:block_count], rest[block_count]
    pairs, pair_width, wide = queries.shape
    half, cells = pair_width // 2, wide // 2
    rows = [block[...].astype(jnp.float32) for block in blocks]
    anchors = jnp.concatenate(rows, axis=0).astype(jnp.bfloat16)
    values = lax.dot_general(
        value_turned[...], anchors, (((1,), (1,)), ((), ())), preferred_element_type=jnp.float32
    ).astype(jnp.bfloat16)
    keys = jnp.dot(anchors, lookup[...], preferred_element_type=jnp.float32).astype(jnp.bfloat16)
    scale = 1.0 / math.sqrt(half)
    spans = [slice(pair * pair_width, (pair + 1) * pair_width) for pair in range(pairs)]
    scores = [
        jnp.dot(keys[:, span], queries[pair], preferred_element_type=jnp.float32)
        for pair, span in enumerate(spans)
    ]
    scores = [score * (multiplier[pair : pair + 1, :] * scale) for pair, score in enumerate(scores)]
    exp_scores = [jnp.exp(score - jnp.max(score, axis=0, keepdims=True)) for score in scores]
    denominators = [jnp.sum(exp_score, axis=0, keepdims=True) for exp_score in exp_scores]
    added = [
        jnp.dot(values[span, :], exp_score.astype(jnp.bfloat16), preferred_element_type=jnp.float32)
        for span, exp_score in zip(spans, exp_scores)
    ]
    context = []
    for pair_added, denominator in zip(added, denominators):
        context.append(pair_added[:half, :cells] / denominator[:, :cells])
        context.append(pair_added[half:, cells:] / denominator[:, cells:])
    terms[...] = lax.dot_general(
        jnp.concatenate(context, axis=0).astype(jnp.bfloat16),
        final[...],
        (((0,), (0,)), ((), ())),
        preferred_element_type=jnp.float32,
    ).astype(jnp.bfloat16)


def finish_kernel(own, other, update):
    mixed = own[...].astype(jnp.float32) + other[...].astype(jnp.float32)
    factor = lax.rsqrt(jnp.mean(mixed * mixed, axis=1, keepdims=True) + epsilon)
    width = update.shape[1]
    for part in range(mixed.shape[1] // width):

        @pl.when(lax.axis_index("head") == part)
        def _():
            update[...] = (mixed[:, part * width : (part + 1) * width] * factor).astype(update.dtype)


VMEM = pl.BlockSpec(memory_space=pltpu.VMEM)
HBM = pl.BlockSpec(memory_space=pltpu.HBM)
PARAMS = pltpu.CompilerParams(vmem_limit_bytes=32 * 1024 * 1024)


def direct_body(
    shards,
    interior_element_embedding,
    boundary_element_embedding,
    interior_landmark_position,
    boundary_landmark_position,
    interior_rescaling_factor,
    boundary_rescaling_factor,
    question_projection_matrix,
    lookup_projection_matrix,
    content_projection_matrix,
    final_projection_matrix,
    channel_logit_divisor,
):
    cells, width = interior_element_embedding.shape
    local_width = question_projection_matrix.shape[1]
    heads = channel_logit_divisor.shape[0]
    pair_width = 2 * (local_width // heads)
    picks = interior_landmark_position.shape[0] + boundary_landmark_position.shape[0]
    anchors, vol, vol_gain, multiplier = pl.pallas_call(
        anchor_kernel,
        out_shape=(
            jax.ShapeDtypeStruct((picks, width), jnp.bfloat16),
            jax.ShapeDtypeStruct((cells, width), jnp.bfloat16),
            jax.ShapeDtypeStruct((1, width), jnp.float32),
            jax.ShapeDtypeStruct((heads // 2, 2 * cells), jnp.float32),
        ),
        in_specs=[HBM] * 7,
        out_specs=(VMEM,) * 4,
        scratch_shapes=[
            pltpu.SMEM(interior_landmark_position.shape, jnp.int32),
            pltpu.SMEM(boundary_landmark_position.shape, jnp.int32),
            pltpu.VMEM(boundary_element_embedding.shape, jnp.bfloat16),
            pltpu.VMEM((1, width), jnp.float32),
            pltpu.SMEM((heads,), jnp.float32),
            pltpu.SemaphoreType.DMA((7,)),
        ],
        compiler_params=PARAMS,
        cost_estimate=pl.CostEstimate(flops=2*10**10, bytes_accessed=2**20, transcendentals=0),
        name="anchors",
    )(
        *in_hbm(
            interior_landmark_position,
            boundary_landmark_position,
            interior_element_embedding,
            boundary_element_embedding,
            interior_rescaling_factor.reshape(1, width),
            boundary_rescaling_factor.reshape(1, width),
            channel_logit_divisor,
        )
    )
    rounds = [(hop + 1, hop) for hop in range(1, shards - 1, 2)] + [(shards - 1, shards - 1)]
    arrived = [
        lax.ppermute(
            anchors,
            ("tok", "head"),
            [(2 * t + core, 2 * ((t + hop[core]) % shards) + core) for t in range(shards) for core in (0, 1)],
        )
        for hop in rounds[-1:] + rounds[:-1]
    ]
    queries, value_turned = pl.pallas_call(
        query_kernel,
        out_shape=(
            jax.ShapeDtypeStruct((heads // 2, pair_width, 2 * cells), jnp.bfloat16),
            jax.ShapeDtypeStruct((local_width, width), jnp.bfloat16),
        ),
        in_specs=[VMEM] * 6,
        out_specs=(VMEM, VMEM),
        compiler_params=PARAMS,
        cost_estimate=pl.CostEstimate(
            flops=2 * cells * width * local_width, bytes_accessed=8 * width * local_width, transcendentals=0
        ),
        name="queries",
    )(*in_vmem(vol, vol_gain, question_projection_matrix, content_projection_matrix, lookup_projection_matrix, final_projection_matrix))
    swapped = [lax.ppermute(block, "head", [(0, 1), (1, 0)]) for block in arrived[1:]]
    blocks = [anchors, *arrived, *swapped]
    terms = pl.pallas_call(
        functools.partial(attention_kernel, len(blocks)),
        out_shape=jax.ShapeDtypeStruct((cells, width), jnp.bfloat16),
        in_specs=[VMEM] * (5 + len(blocks)),
        out_specs=VMEM,
        compiler_params=PARAMS,
        name="attention",
    )(
        *in_vmem(queries, multiplier, lookup_projection_matrix, value_turned, final_projection_matrix, *blocks),
    )
    other = lax.ppermute(terms, "head", [(0, 1), (1, 0)])
    return pl.pallas_call(
        finish_kernel,
        out_shape=jax.ShapeDtypeStruct((cells, local_width), jnp.bfloat16),
        in_specs=[VMEM, VMEM],
        out_specs=VMEM,
        compiler_params=PARAMS,
        name="finish",
    )(*in_vmem(terms, other))


def solution(mesh):
    placed = (
        P(("groups", "tok"), None),
        P(("groups", "tok"), None),
        P(("groups", "tok")),
        P(("groups", "tok")),
        P(),
        P(),
        P(None, "head"),
        P(None, "head"),
        P(None, "head"),
        P("head", None),
        P("head"),
    )
    shards = mesh.shape["tok"]
    small = shards % 2 == 0 and shards <= 16 and mesh.shape["head"] == 2
    body = functools.partial(direct_body, shards) if small else gathered_body
    return jax.shard_map(
        body, mesh=mesh, in_specs=placed, out_specs=P(("groups", "tok"), "head"), check_vma=False
    )
```

```python
import functools
import math

import jax
import jax.numpy as jnp
from jax import lax
from jax.experimental import pallas as pl
from jax.experimental.pallas import tpu as pltpu
from jax.sharding import PartitionSpec as P

epsilon = 1e-06
key_block = 512


def rms_rows(cells, gain):
    values = cells.astype(jnp.float32)
    mean_square = jnp.mean(values * values, axis=1, keepdims=True)
    return (values * lax.rsqrt(mean_square + epsilon) * gain).astype(jnp.bfloat16)


def absorb(running, key_rows, value_rows, queries, logit_multiplier):
    run_max, denominator, accumulated = running
    parallel_channel_total, channel_dimension, cell_count = queries.shape
    key_heads = key_rows.reshape(key_rows.shape[0], parallel_channel_total, channel_dimension)
    value_heads = value_rows.reshape(value_rows.shape[0], parallel_channel_total, channel_dimension)
    scores = (
        jnp.einsum("jhd,hdc->hjc", key_heads, queries, preferred_element_type=jnp.float32)
        * logit_multiplier
    )
    new_max = jnp.maximum(run_max, jnp.max(scores, axis=1))
    shrink = jnp.exp(run_max - new_max)
    exp_scores = jnp.exp(scores - new_max[:, None, :])
    denominator = denominator * shrink + jnp.sum(exp_scores, axis=1)
    added = jnp.einsum(
        "jhd,hjc->hdc",
        value_heads,
        exp_scores.astype(jnp.bfloat16),
        preferred_element_type=jnp.float32,
    )
    accumulated = accumulated * shrink[:, None, :] + added
    return (new_max, denominator, accumulated)


def make_folder(queries, logit_multiplier):

    def folder(running, shard_rows, offset):
        key_rows, value_rows = shard_rows
        row_count = key_rows.shape[0]
        if row_count > key_block and row_count % key_block == 0:
            row_width = key_rows.shape[1]

            def scan_step(state, key_pair):
                return (absorb(state, key_pair[0], key_pair[1], queries, logit_multiplier), None)

            stacked = (
                key_rows.reshape(row_count // key_block, key_block, row_width),
                value_rows.reshape(row_count // key_block, key_block, row_width),
            )
            running, unused = lax.scan(scan_step, running, stacked)
            return running
        return absorb(running, key_rows, value_rows, queries, logit_multiplier)

    return folder


def project_pair(rows_in, lookup_projection_matrix, content_projection_matrix):
    key_rows = jnp.dot(
        rows_in, lookup_projection_matrix, preferred_element_type=jnp.float32
    ).astype(jnp.bfloat16)
    value_rows = jnp.dot(
        rows_in, content_projection_matrix, preferred_element_type=jnp.float32
    ).astype(jnp.bfloat16)
    return (key_rows, value_rows)


def gathered_body(
    interior_element_embedding,
    boundary_element_embedding,
    interior_landmark_position,
    boundary_landmark_position,
    interior_rescaling_factor,
    boundary_rescaling_factor,
    question_projection_matrix,
    lookup_projection_matrix,
    content_projection_matrix,
    final_projection_matrix,
    channel_logit_divisor,
):
    block_index = lax.axis_index("tok")
    vol_normed = rms_rows(interior_element_embedding, interior_rescaling_factor)
    vol_local = interior_landmark_position - block_index * interior_element_embedding.shape[0]
    surf_local = boundary_landmark_position - block_index * boundary_element_embedding.shape[0]
    vol_picked = jnp.take(vol_normed, vol_local, axis=0)
    surf_picked = rms_rows(
        jnp.take(boundary_element_embedding, surf_local, axis=0), boundary_rescaling_factor
    )
    parallel_channel_total = channel_logit_divisor.shape[0]
    local_width = question_projection_matrix.shape[1]
    channel_dimension = local_width // parallel_channel_total
    cell_count = interior_element_embedding.shape[0]
    query_cols = lax.dot_general(
        question_projection_matrix,
        vol_normed,
        (((0,), (1,)), ((), ())),
        preferred_element_type=jnp.float32,
    )
    queries = query_cols.astype(jnp.bfloat16).reshape(
        parallel_channel_total, channel_dimension, cell_count
    )
    logit_multiplier = (channel_logit_divisor * (1.0 / math.sqrt(channel_dimension)))[:, None, None]
    start_state = (
        jnp.full((parallel_channel_total, cell_count), -1e30, jnp.float32),
        jnp.zeros((parallel_channel_total, cell_count), jnp.float32),
        jnp.zeros((parallel_channel_total, channel_dimension, cell_count), jnp.float32),
    )
    folder = make_folder(queries, logit_multiplier)
    anchors = jnp.concatenate([vol_picked, surf_picked], axis=0)
    anchor_keys, anchor_values = project_pair(
        anchors, lookup_projection_matrix, content_projection_matrix
    )
    final_state = folder(
        start_state,
        (
            lax.all_gather(anchor_keys, "tok", axis=0, tiled=True),
            lax.all_gather(anchor_values, "tok", axis=0, tiled=True),
        ),
        jnp.int32(0),
    )
    run_max, denominator, accumulated = final_state
    context = (
        (accumulated / denominator[:, None, :])
        .astype(jnp.bfloat16)
        .reshape(local_width, cell_count)
    )
    head_terms = lax.dot_general(
        context,
        final_projection_matrix,
        (((0,), (0,)), ((), ())),
        preferred_element_type=jnp.float32,
    )
    full_width = head_terms.shape[1]
    share = lax.psum_scatter(
        head_terms.astype(jnp.bfloat16), "head", scatter_dimension=1, tiled=True
    ).astype(jnp.float32)
    squares = lax.psum(jnp.sum(share * share, axis=1), "head")
    return (share * lax.rsqrt(squares[:, None] / full_width + epsilon)).astype(jnp.bfloat16)


def in_vmem(*arrays):
    return [pltpu.with_memory_space_constraint(array, pltpu.VMEM) for array in arrays]


def in_hbm(*arrays):
    return [pltpu.with_memory_space_constraint(array, pltpu.HBM) for array in arrays]


def normed(values, gain):
    mean_square = jnp.mean(values * values, axis=1, keepdims=True)
    return (values * lax.rsqrt(mean_square + epsilon) * gain).astype(jnp.bfloat16)


def pick_rows(positions, first, cells):
    picks, rows = positions.shape[0], cells.shape[0]
    row = lax.broadcasted_iota(jnp.int32, (picks, rows), 0)
    column = lax.broadcasted_iota(jnp.int32, (picks, rows), 1)
    chosen = jnp.zeros((picks, rows), jnp.int32)
    for pick in range(picks):
        chosen = jnp.where(row == pick, positions[pick] - first, chosen)
    one_hot = jnp.where(chosen == column, 1.0, 0.0).astype(jnp.bfloat16)
    return jnp.dot(one_hot, cells, preferred_element_type=jnp.float32)


def fetch(sources, targets, semaphores):
    copies = [
        pltpu.make_async_copy(source, target, semaphores.at[number])
        for number, (source, target) in enumerate(zip(sources, targets))
    ]
    for copy in copies:
        copy.start()
    return copies


def anchor_kernel(*refs):
    sources, (anchors, vol, vol_gain, multiplier), rest = refs[:7], refs[7:11], refs[11:]
    vol_position, surf_position, surf, surf_gain, divisor, semaphores = rest
    targets = (vol_position, surf_position, vol, surf, vol_gain, surf_gain, divisor)
    for copy in fetch(sources, targets, semaphores):
        copy.wait()
    block_index = lax.axis_index("tok")
    vol_rows = pick_rows(vol_position, block_index * vol.shape[0], vol[...])
    surf_rows = pick_rows(surf_position, block_index * surf.shape[0], surf[...])
    parts = [normed(vol_rows, vol_gain[...]), normed(surf_rows, surf_gain[...])]
    stacked = jnp.concatenate([part.astype(jnp.float32) for part in parts], axis=0)
    anchors[...] = stacked.astype(jnp.bfloat16)
    pairs, wide = multiplier.shape
    left = lax.broadcasted_iota(jnp.int32, (1, wide), 1) < wide // 2
    for pair in range(pairs):
        multiplier[pair : pair + 1, :] = jnp.where(left, divisor[2 * pair], divisor[2 * pair + 1])


def query_kernel(vol, gain, projection, value_projection, lookup, final, queries, value_turned):
    vol_normed = normed(vol[...].astype(jnp.float32), gain[...])
    cells = vol.shape[0]
    columns = lax.dot_general(
        projection[...], vol_normed, (((0,), (1,)), ((), ())), preferred_element_type=jnp.float32
    ).astype(jnp.bfloat16)
    pairs, pair_width, _ = queries.shape
    upper = lax.broadcasted_iota(jnp.int32, (pair_width, cells), 0) < pair_width // 2
    for pair in range(pairs):
        block = columns[pair * pair_width : (pair + 1) * pair_width, :].astype(jnp.float32)
        queries[pair, :, :cells] = jnp.where(upper, block, 0.0).astype(jnp.bfloat16)
        queries[pair, :, cells:] = jnp.where(upper, 0.0, block).astype(jnp.bfloat16)
    value_turned[...] = value_projection[...].T


def attention_kernel(block_count, queries, multiplier, lookup, value_turned, final, *rest):
    blocks, terms = rest[:block_count], rest[block_count]
    pairs, pair_width, wide = queries.shape
    half, cells = pair_width // 2, wide // 2
    rows = [block[...].astype(jnp.float32) for block in blocks]
    anchors = jnp.concatenate(rows, axis=0).astype(jnp.bfloat16)
    values = lax.dot_general(
        value_turned[...], anchors, (((1,), (1,)), ((), ())), preferred_element_type=jnp.float32
    ).astype(jnp.bfloat16)
    keys = jnp.dot(anchors, lookup[...], preferred_element_type=jnp.float32).astype(jnp.bfloat16)
    scale = 1.0 / math.sqrt(half)
    spans = [slice(pair * pair_width, (pair + 1) * pair_width) for pair in range(pairs)]
    scores = [
        jnp.dot(keys[:, span], queries[pair], preferred_element_type=jnp.float32)
        for pair, span in enumerate(spans)
    ]
    scores = [score * (multiplier[pair : pair + 1, :] * scale) for pair, score in enumerate(scores)]
    exp_scores = [jnp.exp(score - jnp.max(score, axis=0, keepdims=True)) for score in scores]
    denominators = [jnp.sum(exp_score, axis=0, keepdims=True) for exp_score in exp_scores]
    added = [
        jnp.dot(values[span, :], exp_score.astype(jnp.bfloat16), preferred_element_type=jnp.float32)
        for span, exp_score in zip(spans, exp_scores)
    ]
    context = []
    for pair_added, denominator in zip(added, denominators):
        context.append(pair_added[:half, :cells] / denominator[:, :cells])
        context.append(pair_added[half:, cells:] / denominator[:, cells:])
    terms[...] = lax.dot_general(
        jnp.concatenate(context, axis=0).astype(jnp.bfloat16),
        final[...],
        (((0,), (0,)), ((), ())),
        preferred_element_type=jnp.float32,
    ).astype(jnp.bfloat16)


def finish_kernel(own, other, update):
    mixed = own[...].astype(jnp.float32) + other[...].astype(jnp.float32)
    factor = lax.rsqrt(jnp.mean(mixed * mixed, axis=1, keepdims=True) + epsilon)
    width = update.shape[1]
    for part in range(mixed.shape[1] // width):

        @pl.when(lax.axis_index("head") == part)
        def _():
            update[...] = (mixed[:, part * width : (part + 1) * width] * factor).astype(update.dtype)


VMEM = pl.BlockSpec(memory_space=pltpu.VMEM)
HBM = pl.BlockSpec(memory_space=pltpu.HBM)
PARAMS = pltpu.CompilerParams(vmem_limit_bytes=32 * 1024 * 1024)


SEARCHED_ROUNDS = [
    ((4, 2, 5, 6, 1, 7, 0, 3), (2, 6, 4, 7, 3, 0, 1, 5)),
    ((1, 7, 3, 5, 0, 2, 4, 6), (5, 4, 7, 1, 6, 3, 2, 0)),
    ((7, 5, 6, 0, 2, 1, 3, 4), (6, 3, 0, 2, 5, 4, 7, 1)),
    ((3, 0, 1, 4, 7, 6, 5, 2), (3, 0, 1, 4, 7, 6, 5, 2)),
]


def permute_rounds(shards):
    if shards == len(SEARCHED_ROUNDS[0][0]):
        return SEARCHED_ROUNDS
    hops = [(hop + 1, hop) for hop in range(1, shards - 1, 2)] + [(shards - 1, shards - 1)]
    return [
        tuple(tuple((t + hop) % shards for t in range(shards)) for hop in pair) for pair in hops
    ]


def direct_body(
    shards,
    interior_element_embedding,
    boundary_element_embedding,
    interior_landmark_position,
    boundary_landmark_position,
    interior_rescaling_factor,
    boundary_rescaling_factor,
    question_projection_matrix,
    lookup_projection_matrix,
    content_projection_matrix,
    final_projection_matrix,
    channel_logit_divisor,
):
    cells, width = interior_element_embedding.shape
    local_width = question_projection_matrix.shape[1]
    heads = channel_logit_divisor.shape[0]
    pair_width = 2 * (local_width // heads)
    picks = interior_landmark_position.shape[0] + boundary_landmark_position.shape[0]
    anchors, vol, vol_gain, multiplier = pl.pallas_call(
        anchor_kernel,
        out_shape=(
            jax.ShapeDtypeStruct((picks, width), jnp.bfloat16),
            jax.ShapeDtypeStruct((cells, width), jnp.bfloat16),
            jax.ShapeDtypeStruct((1, width), jnp.float32),
            jax.ShapeDtypeStruct((heads // 2, 2 * cells), jnp.float32),
        ),
        in_specs=[HBM] * 7,
        out_specs=(VMEM,) * 4,
        scratch_shapes=[
            pltpu.SMEM(interior_landmark_position.shape, jnp.int32),
            pltpu.SMEM(boundary_landmark_position.shape, jnp.int32),
            pltpu.VMEM(boundary_element_embedding.shape, jnp.bfloat16),
            pltpu.VMEM((1, width), jnp.float32),
            pltpu.SMEM((heads,), jnp.float32),
            pltpu.SemaphoreType.DMA((7,)),
        ],
        compiler_params=PARAMS,
        cost_estimate=pl.CostEstimate(flops=2*10**10, bytes_accessed=2**20, transcendentals=0),
        name="anchors",
    )(
        *in_hbm(
            interior_landmark_position,
            boundary_landmark_position,
            interior_element_embedding,
            boundary_element_embedding,
            interior_rescaling_factor.reshape(1, width),
            boundary_rescaling_factor.reshape(1, width),
            channel_logit_divisor,
        )
    )
    rounds = permute_rounds(shards)
    arrived = [
        lax.ppermute(
            anchors,
            ("tok", "head"),
            [(2 * t + core, 2 * targets[core][t] + core) for t in range(shards) for core in (0, 1)],
        )
        for targets in rounds[-1:] + rounds[:-1]
    ]
    queries, value_turned = pl.pallas_call(
        query_kernel,
        out_shape=(
            jax.ShapeDtypeStruct((heads // 2, pair_width, 2 * cells), jnp.bfloat16),
            jax.ShapeDtypeStruct((local_width, width), jnp.bfloat16),
        ),
        in_specs=[VMEM] * 6,
        out_specs=(VMEM, VMEM),
        compiler_params=PARAMS,
        cost_estimate=pl.CostEstimate(
            flops=2 * cells * width * local_width, bytes_accessed=8 * width * local_width, transcendentals=0
        ),
        name="queries",
    )(*in_vmem(vol, vol_gain, question_projection_matrix, content_projection_matrix, lookup_projection_matrix, final_projection_matrix))
    swapped = [lax.ppermute(block, "head", [(0, 1), (1, 0)]) for block in arrived[1:]]
    blocks = [anchors, *arrived, *swapped]
    terms = pl.pallas_call(
        functools.partial(attention_kernel, len(blocks)),
        out_shape=jax.ShapeDtypeStruct((cells, width), jnp.bfloat16),
        in_specs=[VMEM] * (5 + len(blocks)),
        out_specs=VMEM,
        compiler_params=PARAMS,
        name="attention",
    )(
        *in_vmem(queries, multiplier, lookup_projection_matrix, value_turned, final_projection_matrix, *blocks),
    )
    other = lax.ppermute(terms, "head", [(0, 1), (1, 0)])
    return pl.pallas_call(
        finish_kernel,
        out_shape=jax.ShapeDtypeStruct((cells, local_width), jnp.bfloat16),
        in_specs=[VMEM, VMEM],
        out_specs=VMEM,
        compiler_params=PARAMS,
        name="finish",
    )(*in_vmem(terms, other))


def solution(mesh):
    placed = (
        P(("groups", "tok"), None),
        P(("groups", "tok"), None),
        P(("groups", "tok")),
        P(("groups", "tok")),
        P(),
        P(),
        P(None, "head"),
        P(None, "head"),
        P(None, "head"),
        P("head", None),
        P("head"),
    )
    shards = mesh.shape["tok"]
    small = shards % 2 == 0 and shards <= 16 and mesh.shape["head"] == 2
    body = functools.partial(direct_body, shards) if small else gathered_body
    return jax.shard_map(
        body, mesh=mesh, in_specs=placed, out_specs=P(("groups", "tok"), "head"), check_vma=False
    )
```

```python
import functools
import math

import jax
import jax.numpy as jnp
from jax import lax
from jax.experimental import pallas as pl
from jax.experimental.pallas import tpu as pltpu
from jax.sharding import PartitionSpec as P

epsilon = 1e-06
key_block = 512


def rms_rows(cells, gain):
    values = cells.astype(jnp.float32)
    mean_square = jnp.mean(values * values, axis=1, keepdims=True)
    return (values * lax.rsqrt(mean_square + epsilon) * gain).astype(jnp.bfloat16)


def absorb(running, key_rows, value_rows, queries, logit_multiplier):
    run_max, denominator, accumulated = running
    parallel_channel_total, channel_dimension, cell_count = queries.shape
    key_heads = key_rows.reshape(key_rows.shape[0], parallel_channel_total, channel_dimension)
    value_heads = value_rows.reshape(value_rows.shape[0], parallel_channel_total, channel_dimension)
    scores = (
        jnp.einsum("jhd,hdc->hjc", key_heads, queries, preferred_element_type=jnp.float32)
        * logit_multiplier
    )
    new_max = jnp.maximum(run_max, jnp.max(scores, axis=1))
    shrink = jnp.exp(run_max - new_max)
    exp_scores = jnp.exp(scores - new_max[:, None, :])
    denominator = denominator * shrink + jnp.sum(exp_scores, axis=1)
    added = jnp.einsum(
        "jhd,hjc->hdc",
        value_heads,
        exp_scores.astype(jnp.bfloat16),
        preferred_element_type=jnp.float32,
    )
    accumulated = accumulated * shrink[:, None, :] + added
    return (new_max, denominator, accumulated)


def make_folder(queries, logit_multiplier):

    def folder(running, shard_rows, offset):
        key_rows, value_rows = shard_rows
        row_count = key_rows.shape[0]
        if row_count > key_block and row_count % key_block == 0:
            row_width = key_rows.shape[1]

            def scan_step(state, key_pair):
                return (absorb(state, key_pair[0], key_pair[1], queries, logit_multiplier), None)

            stacked = (
                key_rows.reshape(row_count // key_block, key_block, row_width),
                value_rows.reshape(row_count // key_block, key_block, row_width),
            )
            running, unused = lax.scan(scan_step, running, stacked)
            return running
        return absorb(running, key_rows, value_rows, queries, logit_multiplier)

    return folder


def project_pair(rows_in, lookup_projection_matrix, content_projection_matrix):
    key_rows = jnp.dot(
        rows_in, lookup_projection_matrix, preferred_element_type=jnp.float32
    ).astype(jnp.bfloat16)
    value_rows = jnp.dot(
        rows_in, content_projection_matrix, preferred_element_type=jnp.float32
    ).astype(jnp.bfloat16)
    return (key_rows, value_rows)


def gathered_body(
    interior_element_embedding,
    boundary_element_embedding,
    interior_landmark_position,
    boundary_landmark_position,
    interior_rescaling_factor,
    boundary_rescaling_factor,
    question_projection_matrix,
    lookup_projection_matrix,
    content_projection_matrix,
    final_projection_matrix,
    channel_logit_divisor,
):
    block_index = lax.axis_index("tok")
    vol_normed = rms_rows(interior_element_embedding, interior_rescaling_factor)
    vol_local = interior_landmark_position - block_index * interior_element_embedding.shape[0]
    surf_local = boundary_landmark_position - block_index * boundary_element_embedding.shape[0]
    vol_picked = jnp.take(vol_normed, vol_local, axis=0)
    surf_picked = rms_rows(
        jnp.take(boundary_element_embedding, surf_local, axis=0), boundary_rescaling_factor
    )
    parallel_channel_total = channel_logit_divisor.shape[0]
    local_width = question_projection_matrix.shape[1]
    channel_dimension = local_width // parallel_channel_total
    cell_count = interior_element_embedding.shape[0]
    query_cols = lax.dot_general(
        question_projection_matrix,
        vol_normed,
        (((0,), (1,)), ((), ())),
        preferred_element_type=jnp.float32,
    )
    queries = query_cols.astype(jnp.bfloat16).reshape(
        parallel_channel_total, channel_dimension, cell_count
    )
    logit_multiplier = (channel_logit_divisor * (1.0 / math.sqrt(channel_dimension)))[:, None, None]
    start_state = (
        jnp.full((parallel_channel_total, cell_count), -1e30, jnp.float32),
        jnp.zeros((parallel_channel_total, cell_count), jnp.float32),
        jnp.zeros((parallel_channel_total, channel_dimension, cell_count), jnp.float32),
    )
    folder = make_folder(queries, logit_multiplier)
    anchors = jnp.concatenate([vol_picked, surf_picked], axis=0)
    anchor_keys, anchor_values = project_pair(
        anchors, lookup_projection_matrix, content_projection_matrix
    )
    final_state = folder(
        start_state,
        (
            lax.all_gather(anchor_keys, "tok", axis=0, tiled=True),
            lax.all_gather(anchor_values, "tok", axis=0, tiled=True),
        ),
        jnp.int32(0),
    )
    run_max, denominator, accumulated = final_state
    context = (
        (accumulated / denominator[:, None, :])
        .astype(jnp.bfloat16)
        .reshape(local_width, cell_count)
    )
    head_terms = lax.dot_general(
        context,
        final_projection_matrix,
        (((0,), (0,)), ((), ())),
        preferred_element_type=jnp.float32,
    )
    full_width = head_terms.shape[1]
    share = lax.psum_scatter(
        head_terms.astype(jnp.bfloat16), "head", scatter_dimension=1, tiled=True
    ).astype(jnp.float32)
    squares = lax.psum(jnp.sum(share * share, axis=1), "head")
    return (share * lax.rsqrt(squares[:, None] / full_width + epsilon)).astype(jnp.bfloat16)


def in_vmem(*arrays):
    return [pltpu.with_memory_space_constraint(array, pltpu.VMEM) for array in arrays]


def in_hbm(*arrays):
    return [pltpu.with_memory_space_constraint(array, pltpu.HBM) for array in arrays]


def normed(values, gain):
    mean_square = jnp.mean(values * values, axis=1, keepdims=True)
    return (values * lax.rsqrt(mean_square + epsilon) * gain).astype(jnp.bfloat16)


def pick_rows(positions, first, cells):
    picks, rows = positions.shape[0], cells.shape[0]
    row = lax.broadcasted_iota(jnp.int32, (picks, rows), 0)
    column = lax.broadcasted_iota(jnp.int32, (picks, rows), 1)
    chosen = jnp.zeros((picks, rows), jnp.int32)
    for pick in range(picks):
        chosen = jnp.where(row == pick, positions[pick] - first, chosen)
    one_hot = jnp.where(chosen == column, 1.0, 0.0).astype(jnp.bfloat16)
    return jnp.dot(one_hot, cells, preferred_element_type=jnp.float32)


def fetch(sources, targets, semaphores):
    copies = [
        pltpu.make_async_copy(source, target, semaphores.at[number])
        for number, (source, target) in enumerate(zip(sources, targets))
    ]
    for copy in copies:
        copy.start()
    return copies


def anchor_kernel(*refs):
    sources, (anchors, vol, vol_gain, multiplier), rest = refs[:7], refs[7:11], refs[11:]
    vol_position, surf_position, surf, surf_gain, divisor, semaphores = rest
    targets = (vol_position, surf_position, vol, surf, vol_gain, surf_gain, divisor)
    for copy in fetch(sources, targets, semaphores):
        copy.wait()
    block_index = lax.axis_index("tok")
    vol_rows = pick_rows(vol_position, block_index * vol.shape[0], vol[...])
    surf_rows = pick_rows(surf_position, block_index * surf.shape[0], surf[...])
    parts = [normed(vol_rows, vol_gain[...]), normed(surf_rows, surf_gain[...])]
    stacked = jnp.concatenate([part.astype(jnp.float32) for part in parts], axis=0)
    anchors[...] = stacked.astype(jnp.bfloat16)
    pairs, wide = multiplier.shape
    left = lax.broadcasted_iota(jnp.int32, (1, wide), 1) < wide // 2
    for pair in range(pairs):
        multiplier[pair : pair + 1, :] = jnp.where(left, divisor[2 * pair], divisor[2 * pair + 1])


def query_kernel(vol, gain, projection, value_projection, lookup, final, queries, value_turned):
    vol_normed = normed(vol[...].astype(jnp.float32), gain[...])
    cells = vol.shape[0]
    columns = lax.dot_general(
        projection[...], vol_normed, (((0,), (1,)), ((), ())), preferred_element_type=jnp.float32
    ).astype(jnp.bfloat16)
    pairs, pair_width, _ = queries.shape
    upper = lax.broadcasted_iota(jnp.int32, (pair_width, cells), 0) < pair_width // 2
    for pair in range(pairs):
        block = columns[pair * pair_width : (pair + 1) * pair_width, :].astype(jnp.float32)
        queries[pair, :, :cells] = jnp.where(upper, block, 0.0).astype(jnp.bfloat16)
        queries[pair, :, cells:] = jnp.where(upper, 0.0, block).astype(jnp.bfloat16)
    value_turned[...] = value_projection[...].T


def attention_kernel(block_count, queries, multiplier, lookup, value_turned, final, *rest):
    blocks, terms = rest[:block_count], rest[block_count]
    pairs, pair_width, wide = queries.shape
    half, cells = pair_width // 2, wide // 2
    rows = [block[...].astype(jnp.float32) for block in blocks]
    anchors = jnp.concatenate(rows, axis=0).astype(jnp.bfloat16)
    values = lax.dot_general(
        value_turned[...], anchors, (((1,), (1,)), ((), ())), preferred_element_type=jnp.float32
    ).astype(jnp.bfloat16)
    keys = jnp.dot(anchors, lookup[...], preferred_element_type=jnp.float32).astype(jnp.bfloat16)
    scale = 1.0 / math.sqrt(half)
    spans = [slice(pair * pair_width, (pair + 1) * pair_width) for pair in range(pairs)]
    scores = [
        jnp.dot(keys[:, span], queries[pair], preferred_element_type=jnp.float32)
        for pair, span in enumerate(spans)
    ]
    scores = [score * (multiplier[pair : pair + 1, :] * scale) for pair, score in enumerate(scores)]
    exp_scores = [jnp.exp(score - jnp.max(score, axis=0, keepdims=True)) for score in scores]
    denominators = [jnp.sum(exp_score, axis=0, keepdims=True) for exp_score in exp_scores]
    added = [
        jnp.dot(values[span, :], exp_score.astype(jnp.bfloat16), preferred_element_type=jnp.float32)
        for span, exp_score in zip(spans, exp_scores)
    ]
    context = []
    for pair_added, denominator in zip(added, denominators):
        context.append(pair_added[:half, :cells] / denominator[:, :cells])
        context.append(pair_added[half:, cells:] / denominator[:, cells:])
    terms[...] = lax.dot_general(
        jnp.concatenate(context, axis=0).astype(jnp.bfloat16),
        final[...],
        (((0,), (0,)), ((), ())),
        preferred_element_type=jnp.float32,
    ).astype(jnp.bfloat16)


def finish_kernel(own, other, update):
    mixed = own[...].astype(jnp.float32) + other[...].astype(jnp.float32)
    factor = lax.rsqrt(jnp.mean(mixed * mixed, axis=1, keepdims=True) + epsilon)
    width = update.shape[1]
    for part in range(mixed.shape[1] // width):

        @pl.when(lax.axis_index("head") == part)
        def _():
            update[...] = (mixed[:, part * width : (part + 1) * width] * factor).astype(update.dtype)


VMEM = pl.BlockSpec(memory_space=pltpu.VMEM)
HBM = pl.BlockSpec(memory_space=pltpu.HBM)
PARAMS = pltpu.CompilerParams(vmem_limit_bytes=32 * 1024 * 1024)


SEARCHED_ROUNDS = [
    (7, 2, 11, 8, 9, 6, 10, 13, 5, 14, 15, 0, 4, 3, 12, 1),
    (11, 8, 15, 4, 13, 2, 14, 9, 0, 3, 7, 12, 1, 10, 6, 5),
    (5, 12, 7, 0, 11, 14, 1, 2, 13, 6, 4, 9, 8, 15, 3, 10),
    (14, 15, 13, 12, 1, 0, 4, 5, 10, 11, 3, 2, 6, 7, 9, 8),
]


def permute_rounds(shards):
    if 2 * shards == len(SEARCHED_ROUNDS[0]):
        return SEARCHED_ROUNDS
    hops = [(hop + 1, hop) for hop in range(1, shards - 1, 2)] + [(shards - 1, shards - 1)]
    return [
        tuple(2 * ((t + pair[core]) % shards) + core for t in range(shards) for core in (0, 1))
        for pair in hops
    ]


def direct_body(
    shards,
    interior_element_embedding,
    boundary_element_embedding,
    interior_landmark_position,
    boundary_landmark_position,
    interior_rescaling_factor,
    boundary_rescaling_factor,
    question_projection_matrix,
    lookup_projection_matrix,
    content_projection_matrix,
    final_projection_matrix,
    channel_logit_divisor,
):
    cells, width = interior_element_embedding.shape
    local_width = question_projection_matrix.shape[1]
    heads = channel_logit_divisor.shape[0]
    pair_width = 2 * (local_width // heads)
    picks = interior_landmark_position.shape[0] + boundary_landmark_position.shape[0]
    anchors, vol, vol_gain, multiplier = pl.pallas_call(
        anchor_kernel,
        out_shape=(
            jax.ShapeDtypeStruct((picks, width), jnp.bfloat16),
            jax.ShapeDtypeStruct((cells, width), jnp.bfloat16),
            jax.ShapeDtypeStruct((1, width), jnp.float32),
            jax.ShapeDtypeStruct((heads // 2, 2 * cells), jnp.float32),
        ),
        in_specs=[HBM] * 7,
        out_specs=(VMEM,) * 4,
        scratch_shapes=[
            pltpu.SMEM(interior_landmark_position.shape, jnp.int32),
            pltpu.SMEM(boundary_landmark_position.shape, jnp.int32),
            pltpu.VMEM(boundary_element_embedding.shape, jnp.bfloat16),
            pltpu.VMEM((1, width), jnp.float32),
            pltpu.SMEM((heads,), jnp.float32),
            pltpu.SemaphoreType.DMA((7,)),
        ],
        compiler_params=PARAMS,
        cost_estimate=pl.CostEstimate(flops=2*10**10, bytes_accessed=2**20, transcendentals=0),
        name="anchors",
    )(
        *in_hbm(
            interior_landmark_position,
            boundary_landmark_position,
            interior_element_embedding,
            boundary_element_embedding,
            interior_rescaling_factor.reshape(1, width),
            boundary_rescaling_factor.reshape(1, width),
            channel_logit_divisor,
        )
    )
    rounds = permute_rounds(shards)
    arrived = [
        lax.ppermute(anchors, ("tok", "head"), list(enumerate(targets)))
        for targets in rounds[-1:] + rounds[:-1]
    ]
    queries, value_turned = pl.pallas_call(
        query_kernel,
        out_shape=(
            jax.ShapeDtypeStruct((heads // 2, pair_width, 2 * cells), jnp.bfloat16),
            jax.ShapeDtypeStruct((local_width, width), jnp.bfloat16),
        ),
        in_specs=[VMEM] * 6,
        out_specs=(VMEM, VMEM),
        compiler_params=PARAMS,
        cost_estimate=pl.CostEstimate(
            flops=2 * cells * width * local_width, bytes_accessed=8 * width * local_width, transcendentals=0
        ),
        name="queries",
    )(*in_vmem(vol, vol_gain, question_projection_matrix, content_projection_matrix, lookup_projection_matrix, final_projection_matrix))
    swapped = [lax.ppermute(block, "head", [(0, 1), (1, 0)]) for block in arrived[1:]]
    blocks = [anchors, *arrived, *swapped]
    terms = pl.pallas_call(
        functools.partial(attention_kernel, len(blocks)),
        out_shape=jax.ShapeDtypeStruct((cells, width), jnp.bfloat16),
        in_specs=[VMEM] * (5 + len(blocks)),
        out_specs=VMEM,
        compiler_params=PARAMS,
        name="attention",
    )(
        *in_vmem(queries, multiplier, lookup_projection_matrix, value_turned, final_projection_matrix, *blocks),
    )
    other = lax.ppermute(terms, "head", [(0, 1), (1, 0)])
    return pl.pallas_call(
        finish_kernel,
        out_shape=jax.ShapeDtypeStruct((cells, local_width), jnp.bfloat16),
        in_specs=[VMEM, VMEM],
        out_specs=VMEM,
        compiler_params=PARAMS,
        name="finish",
    )(*in_vmem(terms, other))


def solution(mesh):
    placed = (
        P(("groups", "tok"), None),
        P(("groups", "tok"), None),
        P(("groups", "tok")),
        P(("groups", "tok")),
        P(),
        P(),
        P(None, "head"),
        P(None, "head"),
        P(None, "head"),
        P("head", None),
        P("head"),
    )
    shards = mesh.shape["tok"]
    small = shards % 2 == 0 and shards <= 16 and mesh.shape["head"] == 2
    body = functools.partial(direct_body, shards) if small else gathered_body
    return jax.shard_map(
        body, mesh=mesh, in_specs=placed, out_specs=P(("groups", "tok"), "head"), check_vma=False
    )
```

```python
import functools
import math

import jax
import jax.numpy as jnp
from jax import lax
from jax.experimental import pallas as pl
from jax.experimental.pallas import tpu as pltpu
from jax.sharding import PartitionSpec as P

epsilon = 1e-06
key_block = 512


def rms_rows(cells, gain):
    values = cells.astype(jnp.float32)
    mean_square = jnp.mean(values * values, axis=1, keepdims=True)
    return (values * lax.rsqrt(mean_square + epsilon) * gain).astype(jnp.bfloat16)


def absorb(running, key_rows, value_rows, queries, logit_multiplier):
    run_max, denominator, accumulated = running
    parallel_channel_total, channel_dimension, cell_count = queries.shape
    key_heads = key_rows.reshape(key_rows.shape[0], parallel_channel_total, channel_dimension)
    value_heads = value_rows.reshape(value_rows.shape[0], parallel_channel_total, channel_dimension)
    scores = (
        jnp.einsum("jhd,hdc->hjc", key_heads, queries, preferred_element_type=jnp.float32)
        * logit_multiplier
    )
    new_max = jnp.maximum(run_max, jnp.max(scores, axis=1))
    shrink = jnp.exp(run_max - new_max)
    exp_scores = jnp.exp(scores - new_max[:, None, :])
    denominator = denominator * shrink + jnp.sum(exp_scores, axis=1)
    added = jnp.einsum(
        "jhd,hjc->hdc",
        value_heads,
        exp_scores.astype(jnp.bfloat16),
        preferred_element_type=jnp.float32,
    )
    accumulated = accumulated * shrink[:, None, :] + added
    return (new_max, denominator, accumulated)


def make_folder(queries, logit_multiplier):

    def folder(running, shard_rows, offset):
        key_rows, value_rows = shard_rows
        row_count = key_rows.shape[0]
        if row_count > key_block and row_count % key_block == 0:
            row_width = key_rows.shape[1]

            def scan_step(state, key_pair):
                return (absorb(state, key_pair[0], key_pair[1], queries, logit_multiplier), None)

            stacked = (
                key_rows.reshape(row_count // key_block, key_block, row_width),
                value_rows.reshape(row_count // key_block, key_block, row_width),
            )
            running, unused = lax.scan(scan_step, running, stacked)
            return running
        return absorb(running, key_rows, value_rows, queries, logit_multiplier)

    return folder


def project_pair(rows_in, lookup_projection_matrix, content_projection_matrix):
    key_rows = jnp.dot(
        rows_in, lookup_projection_matrix, preferred_element_type=jnp.float32
    ).astype(jnp.bfloat16)
    value_rows = jnp.dot(
        rows_in, content_projection_matrix, preferred_element_type=jnp.float32
    ).astype(jnp.bfloat16)
    return (key_rows, value_rows)


def gathered_body(
    interior_element_embedding,
    boundary_element_embedding,
    interior_landmark_position,
    boundary_landmark_position,
    interior_rescaling_factor,
    boundary_rescaling_factor,
    question_projection_matrix,
    lookup_projection_matrix,
    content_projection_matrix,
    final_projection_matrix,
    channel_logit_divisor,
):
    block_index = lax.axis_index("tok")
    vol_normed = rms_rows(interior_element_embedding, interior_rescaling_factor)
    vol_local = interior_landmark_position - block_index * interior_element_embedding.shape[0]
    surf_local = boundary_landmark_position - block_index * boundary_element_embedding.shape[0]
    vol_picked = jnp.take(vol_normed, vol_local, axis=0)
    surf_picked = rms_rows(
        jnp.take(boundary_element_embedding, surf_local, axis=0), boundary_rescaling_factor
    )
    parallel_channel_total = channel_logit_divisor.shape[0]
    local_width = question_projection_matrix.shape[1]
    channel_dimension = local_width // parallel_channel_total
    cell_count = interior_element_embedding.shape[0]
    query_cols = lax.dot_general(
        question_projection_matrix,
        vol_normed,
        (((0,), (1,)), ((), ())),
        preferred_element_type=jnp.float32,
    )
    queries = query_cols.astype(jnp.bfloat16).reshape(
        parallel_channel_total, channel_dimension, cell_count
    )
    logit_multiplier = (channel_logit_divisor * (1.0 / math.sqrt(channel_dimension)))[:, None, None]
    start_state = (
        jnp.full((parallel_channel_total, cell_count), -1e30, jnp.float32),
        jnp.zeros((parallel_channel_total, cell_count), jnp.float32),
        jnp.zeros((parallel_channel_total, channel_dimension, cell_count), jnp.float32),
    )
    folder = make_folder(queries, logit_multiplier)
    anchors = jnp.concatenate([vol_picked, surf_picked], axis=0)
    anchor_keys, anchor_values = project_pair(
        anchors, lookup_projection_matrix, content_projection_matrix
    )
    final_state = folder(
        start_state,
        (
            lax.all_gather(anchor_keys, "tok", axis=0, tiled=True),
            lax.all_gather(anchor_values, "tok", axis=0, tiled=True),
        ),
        jnp.int32(0),
    )
    run_max, denominator, accumulated = final_state
    context = (
        (accumulated / denominator[:, None, :])
        .astype(jnp.bfloat16)
        .reshape(local_width, cell_count)
    )
    head_terms = lax.dot_general(
        context,
        final_projection_matrix,
        (((0,), (0,)), ((), ())),
        preferred_element_type=jnp.float32,
    )
    full_width = head_terms.shape[1]
    share = lax.psum_scatter(
        head_terms.astype(jnp.bfloat16), "head", scatter_dimension=1, tiled=True
    ).astype(jnp.float32)
    squares = lax.psum(jnp.sum(share * share, axis=1), "head")
    return (share * lax.rsqrt(squares[:, None] / full_width + epsilon)).astype(jnp.bfloat16)


def in_vmem(*arrays):
    return [pltpu.with_memory_space_constraint(array, pltpu.VMEM) for array in arrays]


def in_hbm(*arrays):
    return [pltpu.with_memory_space_constraint(array, pltpu.HBM) for array in arrays]


def normed(values, gain):
    mean_square = jnp.mean(values * values, axis=1, keepdims=True)
    return (values * lax.rsqrt(mean_square + epsilon) * gain).astype(jnp.bfloat16)


def pick_rows(positions, first, cells):
    picks, rows = positions.shape[0], cells.shape[0]
    row = lax.broadcasted_iota(jnp.int32, (picks, rows), 0)
    column = lax.broadcasted_iota(jnp.int32, (picks, rows), 1)
    chosen = jnp.zeros((picks, rows), jnp.int32)
    for pick in range(picks):
        chosen = jnp.where(row == pick, positions[pick] - first, chosen)
    one_hot = jnp.where(chosen == column, 1.0, 0.0).astype(jnp.bfloat16)
    return jnp.dot(one_hot, cells, preferred_element_type=jnp.float32)


def fetch(sources, targets, semaphores):
    copies = [
        pltpu.make_async_copy(source, target, semaphores.at[number])
        for number, (source, target) in enumerate(zip(sources, targets))
    ]
    for copy in copies:
        copy.start()
    return copies


def anchor_kernel(*refs):
    sources, (anchors, vol, vol_gain, multiplier), rest = refs[:7], refs[7:11], refs[11:]
    vol_position, surf_position, surf, surf_gain, divisor, semaphores = rest
    targets = (vol_position, surf_position, vol, surf, vol_gain, surf_gain, divisor)
    for copy in fetch(sources, targets, semaphores):
        copy.wait()
    block_index = lax.axis_index("tok")
    vol_rows = pick_rows(vol_position, block_index * vol.shape[0], vol[...])
    surf_rows = pick_rows(surf_position, block_index * surf.shape[0], surf[...])
    parts = [normed(vol_rows, vol_gain[...]), normed(surf_rows, surf_gain[...])]
    stacked = jnp.concatenate([part.astype(jnp.float32) for part in parts], axis=0)
    anchors[...] = stacked.astype(jnp.bfloat16)
    pairs, wide = multiplier.shape
    left = lax.broadcasted_iota(jnp.int32, (1, wide), 1) < wide // 2
    for pair in range(pairs):
        multiplier[pair : pair + 1, :] = jnp.where(left, divisor[2 * pair], divisor[2 * pair + 1])


def copy_kernel(source, target):
    target[...] = source[...]


def query_kernel(vol, gain, projection, value_projection, lookup, final, queries, value_turned):
    vol_normed = normed(vol[...].astype(jnp.float32), gain[...])
    cells = vol.shape[0]
    columns = lax.dot_general(
        projection[...], vol_normed, (((0,), (1,)), ((), ())), preferred_element_type=jnp.float32
    ).astype(jnp.bfloat16)
    pairs, pair_width, _ = queries.shape
    upper = lax.broadcasted_iota(jnp.int32, (pair_width, cells), 0) < pair_width // 2
    for pair in range(pairs):
        block = columns[pair * pair_width : (pair + 1) * pair_width, :].astype(jnp.float32)
        queries[pair, :, :cells] = jnp.where(upper, block, 0.0).astype(jnp.bfloat16)
        queries[pair, :, cells:] = jnp.where(upper, 0.0, block).astype(jnp.bfloat16)
    value_turned[...] = value_projection[...].T


def attention_kernel(block_count, queries, multiplier, lookup, value_turned, final, *rest):
    blocks, terms = rest[:block_count], rest[block_count]
    pairs, pair_width, wide = queries.shape
    half, cells = pair_width // 2, wide // 2
    rows = [block[...].astype(jnp.float32) for block in blocks]
    anchors = jnp.concatenate(rows, axis=0).astype(jnp.bfloat16)
    values = lax.dot_general(
        value_turned[...], anchors, (((1,), (1,)), ((), ())), preferred_element_type=jnp.float32
    ).astype(jnp.bfloat16)
    keys = jnp.dot(anchors, lookup[...], preferred_element_type=jnp.float32).astype(jnp.bfloat16)
    scale = 1.0 / math.sqrt(half)
    spans = [slice(pair * pair_width, (pair + 1) * pair_width) for pair in range(pairs)]
    scores = [
        jnp.dot(keys[:, span], queries[pair], preferred_element_type=jnp.float32)
        for pair, span in enumerate(spans)
    ]
    scores = [score * (multiplier[pair : pair + 1, :] * scale) for pair, score in enumerate(scores)]
    exp_scores = [jnp.exp(score - jnp.max(score, axis=0, keepdims=True)) for score in scores]
    denominators = [jnp.sum(exp_score, axis=0, keepdims=True) for exp_score in exp_scores]
    added = [
        jnp.dot(values[span, :], exp_score.astype(jnp.bfloat16), preferred_element_type=jnp.float32)
        for span, exp_score in zip(spans, exp_scores)
    ]
    context = []
    for pair_added, denominator in zip(added, denominators):
        context.append(pair_added[:half, :cells] / denominator[:, :cells])
        context.append(pair_added[half:, cells:] / denominator[:, cells:])
    terms[...] = lax.dot_general(
        jnp.concatenate(context, axis=0).astype(jnp.bfloat16),
        final[...],
        (((0,), (0,)), ((), ())),
        preferred_element_type=jnp.float32,
    ).astype(jnp.bfloat16)


def finish_kernel(own, other, update):
    mixed = own[...].astype(jnp.float32) + other[...].astype(jnp.float32)
    factor = lax.rsqrt(jnp.mean(mixed * mixed, axis=1, keepdims=True) + epsilon)
    width = update.shape[1]
    for part in range(mixed.shape[1] // width):

        @pl.when(lax.axis_index("head") == part)
        def _():
            update[...] = (mixed[:, part * width : (part + 1) * width] * factor).astype(update.dtype)


VMEM = pl.BlockSpec(memory_space=pltpu.VMEM)
HBM = pl.BlockSpec(memory_space=pltpu.HBM)
PARAMS = pltpu.CompilerParams(vmem_limit_bytes=32 * 1024 * 1024)


SEARCHED_ROUNDS = [
    (7, 2, 11, 8, 9, 6, 10, 13, 5, 14, 15, 0, 4, 3, 12, 1),
    (11, 8, 15, 4, 13, 2, 14, 9, 0, 3, 7, 12, 1, 10, 6, 5),
    (5, 12, 7, 0, 11, 14, 1, 2, 13, 6, 4, 9, 8, 15, 3, 10),
    (14, 15, 13, 12, 1, 0, 4, 5, 10, 11, 3, 2, 6, 7, 9, 8),
]


def permute_rounds(shards):
    if 2 * shards == len(SEARCHED_ROUNDS[0]):
        return SEARCHED_ROUNDS
    hops = [(hop + 1, hop) for hop in range(1, shards - 1, 2)] + [(shards - 1, shards - 1)]
    return [
        tuple(2 * ((t + pair[core]) % shards) + core for t in range(shards) for core in (0, 1))
        for pair in hops
    ]


def direct_body(
    shards,
    interior_element_embedding,
    boundary_element_embedding,
    interior_landmark_position,
    boundary_landmark_position,
    interior_rescaling_factor,
    boundary_rescaling_factor,
    question_projection_matrix,
    lookup_projection_matrix,
    content_projection_matrix,
    final_projection_matrix,
    channel_logit_divisor,
):
    cells, width = interior_element_embedding.shape
    local_width = question_projection_matrix.shape[1]
    heads = channel_logit_divisor.shape[0]
    pair_width = 2 * (local_width // heads)
    picks = interior_landmark_position.shape[0] + boundary_landmark_position.shape[0]
    anchors, vol, vol_gain, multiplier = pl.pallas_call(
        anchor_kernel,
        out_shape=(
            jax.ShapeDtypeStruct((picks, width), jnp.bfloat16),
            jax.ShapeDtypeStruct((cells, width), jnp.bfloat16),
            jax.ShapeDtypeStruct((1, width), jnp.float32),
            jax.ShapeDtypeStruct((heads // 2, 2 * cells), jnp.float32),
        ),
        in_specs=[HBM] * 7,
        out_specs=(VMEM,) * 4,
        scratch_shapes=[
            pltpu.SMEM(interior_landmark_position.shape, jnp.int32),
            pltpu.SMEM(boundary_landmark_position.shape, jnp.int32),
            pltpu.VMEM(boundary_element_embedding.shape, jnp.bfloat16),
            pltpu.VMEM((1, width), jnp.float32),
            pltpu.SMEM((heads,), jnp.float32),
            pltpu.SemaphoreType.DMA((7,)),
        ],
        compiler_params=PARAMS,
        name="anchors",
    )(
        *in_hbm(
            interior_landmark_position,
            boundary_landmark_position,
            interior_element_embedding,
            boundary_element_embedding,
            interior_rescaling_factor.reshape(1, width),
            boundary_rescaling_factor.reshape(1, width),
            channel_logit_divisor,
        )
    )
    rounds = permute_rounds(shards)
    again = pl.pallas_call(
        copy_kernel,
        out_shape=jax.ShapeDtypeStruct(anchors.shape, anchors.dtype),
        in_specs=[VMEM],
        out_specs=VMEM,
        compiler_params=PARAMS,
        cost_estimate=pl.CostEstimate(flops=2 * 10**10, bytes_accessed=2**16, transcendentals=0),
        name="again",
    )(*in_vmem(anchors))
    arrived = [
        lax.ppermute(sent, ("tok", "head"), list(enumerate(targets)))
        for sent, targets in [(again, rounds[-1])] + [(anchors, targets) for targets in rounds[:-1]]
    ]
    queries, value_turned = pl.pallas_call(
        query_kernel,
        out_shape=(
            jax.ShapeDtypeStruct((heads // 2, pair_width, 2 * cells), jnp.bfloat16),
            jax.ShapeDtypeStruct((local_width, width), jnp.bfloat16),
        ),
        in_specs=[VMEM] * 6,
        out_specs=(VMEM, VMEM),
        compiler_params=PARAMS,
        cost_estimate=pl.CostEstimate(
            flops=2 * cells * width * local_width, bytes_accessed=8 * width * local_width, transcendentals=0
        ),
        name="queries",
    )(*in_vmem(vol, vol_gain, question_projection_matrix, content_projection_matrix, lookup_projection_matrix, final_projection_matrix))
    swapped = [lax.ppermute(block, "head", [(0, 1), (1, 0)]) for block in arrived[1:]]
    blocks = [anchors, *arrived, *swapped]
    terms = pl.pallas_call(
        functools.partial(attention_kernel, len(blocks)),
        out_shape=jax.ShapeDtypeStruct((cells, width), jnp.bfloat16),
        in_specs=[VMEM] * (5 + len(blocks)),
        out_specs=VMEM,
        compiler_params=PARAMS,
        name="attention",
    )(
        *in_vmem(queries, multiplier, lookup_projection_matrix, value_turned, final_projection_matrix, *blocks),
    )
    other = lax.ppermute(terms, "head", [(0, 1), (1, 0)])
    return pl.pallas_call(
        finish_kernel,
        out_shape=jax.ShapeDtypeStruct((cells, local_width), jnp.bfloat16),
        in_specs=[VMEM, VMEM],
        out_specs=VMEM,
        compiler_params=PARAMS,
        name="finish",
    )(*in_vmem(terms, other))


def solution(mesh):
    placed = (
        P(("groups", "tok"), None),
        P(("groups", "tok"), None),
        P(("groups", "tok")),
        P(("groups", "tok")),
        P(),
        P(),
        P(None, "head"),
        P(None, "head"),
        P(None, "head"),
        P("head", None),
        P("head"),
    )
    shards = mesh.shape["tok"]
    small = shards % 2 == 0 and shards <= 16 and mesh.shape["head"] == 2
    body = functools.partial(direct_body, shards) if small else gathered_body
    return jax.shard_map(
        body, mesh=mesh, in_specs=placed, out_specs=P(("groups", "tok"), "head"), check_vma=False
    )
```

```python
import functools
import math

import jax
import jax.numpy as jnp
from jax import lax
from jax.experimental import pallas as pl
from jax.experimental.pallas import tpu as pltpu
from jax.sharding import PartitionSpec as P

epsilon = 1e-06
key_block = 512


def rms_rows(cells, gain):
    values = cells.astype(jnp.float32)
    mean_square = jnp.mean(values * values, axis=1, keepdims=True)
    return (values * lax.rsqrt(mean_square + epsilon) * gain).astype(jnp.bfloat16)


def absorb(running, key_rows, value_rows, queries, logit_multiplier):
    run_max, denominator, accumulated = running
    parallel_channel_total, channel_dimension, cell_count = queries.shape
    key_heads = key_rows.reshape(key_rows.shape[0], parallel_channel_total, channel_dimension)
    value_heads = value_rows.reshape(value_rows.shape[0], parallel_channel_total, channel_dimension)
    scores = (
        jnp.einsum("jhd,hdc->hjc", key_heads, queries, preferred_element_type=jnp.float32)
        * logit_multiplier
    )
    new_max = jnp.maximum(run_max, jnp.max(scores, axis=1))
    shrink = jnp.exp(run_max - new_max)
    exp_scores = jnp.exp(scores - new_max[:, None, :])
    denominator = denominator * shrink + jnp.sum(exp_scores, axis=1)
    added = jnp.einsum(
        "jhd,hjc->hdc",
        value_heads,
        exp_scores.astype(jnp.bfloat16),
        preferred_element_type=jnp.float32,
    )
    accumulated = accumulated * shrink[:, None, :] + added
    return (new_max, denominator, accumulated)


def make_folder(queries, logit_multiplier):

    def folder(running, shard_rows, offset):
        key_rows, value_rows = shard_rows
        row_count = key_rows.shape[0]
        if row_count > key_block and row_count % key_block == 0:
            row_width = key_rows.shape[1]

            def scan_step(state, key_pair):
                return (absorb(state, key_pair[0], key_pair[1], queries, logit_multiplier), None)

            stacked = (
                key_rows.reshape(row_count // key_block, key_block, row_width),
                value_rows.reshape(row_count // key_block, key_block, row_width),
            )
            running, unused = lax.scan(scan_step, running, stacked)
            return running
        return absorb(running, key_rows, value_rows, queries, logit_multiplier)

    return folder


def project_pair(rows_in, lookup_projection_matrix, content_projection_matrix):
    key_rows = jnp.dot(
        rows_in, lookup_projection_matrix, preferred_element_type=jnp.float32
    ).astype(jnp.bfloat16)
    value_rows = jnp.dot(
        rows_in, content_projection_matrix, preferred_element_type=jnp.float32
    ).astype(jnp.bfloat16)
    return (key_rows, value_rows)


def gathered_body(
    interior_element_embedding,
    boundary_element_embedding,
    interior_landmark_position,
    boundary_landmark_position,
    interior_rescaling_factor,
    boundary_rescaling_factor,
    question_projection_matrix,
    lookup_projection_matrix,
    content_projection_matrix,
    final_projection_matrix,
    channel_logit_divisor,
):
    block_index = lax.axis_index("tok")
    vol_normed = rms_rows(interior_element_embedding, interior_rescaling_factor)
    vol_local = interior_landmark_position - block_index * interior_element_embedding.shape[0]
    surf_local = boundary_landmark_position - block_index * boundary_element_embedding.shape[0]
    vol_picked = jnp.take(vol_normed, vol_local, axis=0)
    surf_picked = rms_rows(
        jnp.take(boundary_element_embedding, surf_local, axis=0), boundary_rescaling_factor
    )
    parallel_channel_total = channel_logit_divisor.shape[0]
    local_width = question_projection_matrix.shape[1]
    channel_dimension = local_width // parallel_channel_total
    cell_count = interior_element_embedding.shape[0]
    query_cols = lax.dot_general(
        question_projection_matrix,
        vol_normed,
        (((0,), (1,)), ((), ())),
        preferred_element_type=jnp.float32,
    )
    queries = query_cols.astype(jnp.bfloat16).reshape(
        parallel_channel_total, channel_dimension, cell_count
    )
    logit_multiplier = (channel_logit_divisor * (1.0 / math.sqrt(channel_dimension)))[:, None, None]
    start_state = (
        jnp.full((parallel_channel_total, cell_count), -1e30, jnp.float32),
        jnp.zeros((parallel_channel_total, cell_count), jnp.float32),
        jnp.zeros((parallel_channel_total, channel_dimension, cell_count), jnp.float32),
    )
    folder = make_folder(queries, logit_multiplier)
    anchors = jnp.concatenate([vol_picked, surf_picked], axis=0)
    anchor_keys, anchor_values = project_pair(
        anchors, lookup_projection_matrix, content_projection_matrix
    )
    final_state = folder(
        start_state,
        (
            lax.all_gather(anchor_keys, "tok", axis=0, tiled=True),
            lax.all_gather(anchor_values, "tok", axis=0, tiled=True),
        ),
        jnp.int32(0),
    )
    run_max, denominator, accumulated = final_state
    context = (
        (accumulated / denominator[:, None, :])
        .astype(jnp.bfloat16)
        .reshape(local_width, cell_count)
    )
    head_terms = lax.dot_general(
        context,
        final_projection_matrix,
        (((0,), (0,)), ((), ())),
        preferred_element_type=jnp.float32,
    )
    full_width = head_terms.shape[1]
    share = lax.psum_scatter(
        head_terms.astype(jnp.bfloat16), "head", scatter_dimension=1, tiled=True
    ).astype(jnp.float32)
    squares = lax.psum(jnp.sum(share * share, axis=1), "head")
    return (share * lax.rsqrt(squares[:, None] / full_width + epsilon)).astype(jnp.bfloat16)


def in_vmem(*arrays):
    return [pltpu.with_memory_space_constraint(array, pltpu.VMEM) for array in arrays]


def in_hbm(*arrays):
    return [pltpu.with_memory_space_constraint(array, pltpu.HBM) for array in arrays]


def normed(values, gain):
    mean_square = jnp.mean(values * values, axis=1, keepdims=True)
    return (values * lax.rsqrt(mean_square + epsilon) * gain).astype(jnp.bfloat16)


def pick_rows(positions, first, cells):
    picks, rows = positions.shape[0], cells.shape[0]
    row = lax.broadcasted_iota(jnp.int32, (picks, rows), 0)
    column = lax.broadcasted_iota(jnp.int32, (picks, rows), 1)
    chosen = jnp.zeros((picks, rows), jnp.int32)
    for pick in range(picks):
        chosen = jnp.where(row == pick, positions[pick] - first, chosen)
    one_hot = jnp.where(chosen == column, 1.0, 0.0).astype(jnp.bfloat16)
    return jnp.dot(one_hot, cells, preferred_element_type=jnp.float32)


def fetch(sources, targets, semaphores):
    copies = [
        pltpu.make_async_copy(source, target, semaphores.at[number])
        for number, (source, target) in enumerate(zip(sources, targets))
    ]
    for copy in copies:
        copy.start()
    return copies


def anchor_kernel(*refs):
    sources, (anchors, vol, vol_gain, multiplier), rest = refs[:7], refs[7:11], refs[11:]
    vol_position, surf_position, surf, surf_gain, divisor, semaphores = rest
    targets = (vol_position, surf_position, vol, surf, vol_gain, surf_gain, divisor)
    for copy in fetch(sources, targets, semaphores):
        copy.wait()
    block_index = lax.axis_index("tok")
    vol_rows = pick_rows(vol_position, block_index * vol.shape[0], vol[...])
    surf_rows = pick_rows(surf_position, block_index * surf.shape[0], surf[...])
    parts = [normed(vol_rows, vol_gain[...]), normed(surf_rows, surf_gain[...])]
    stacked = jnp.concatenate([part.astype(jnp.float32) for part in parts], axis=0)
    anchors[...] = stacked.astype(jnp.bfloat16)
    pairs, wide = multiplier.shape
    left = lax.broadcasted_iota(jnp.int32, (1, wide), 1) < wide // 2
    for pair in range(pairs):
        multiplier[pair : pair + 1, :] = jnp.where(left, divisor[2 * pair], divisor[2 * pair + 1])


def copy_kernel(source, target):
    target[...] = source[...]


def query_kernel(vol, gain, projection, value_projection, lookup, final, queries, value_turned):
    vol_normed = normed(vol[...].astype(jnp.float32), gain[...])
    cells = vol.shape[0]
    columns = lax.dot_general(
        projection[...], vol_normed, (((0,), (1,)), ((), ())), preferred_element_type=jnp.float32
    ).astype(jnp.bfloat16)
    pairs, pair_width, _ = queries.shape
    upper = lax.broadcasted_iota(jnp.int32, (pair_width, cells), 0) < pair_width // 2
    for pair in range(pairs):
        block = columns[pair * pair_width : (pair + 1) * pair_width, :].astype(jnp.float32)
        queries[pair, :, :cells] = jnp.where(upper, block, 0.0).astype(jnp.bfloat16)
        queries[pair, :, cells:] = jnp.where(upper, 0.0, block).astype(jnp.bfloat16)
    value_turned[...] = value_projection[...].T


def attention_kernel(block_count, queries, multiplier, lookup, value_turned, final, *rest):
    blocks, terms = rest[:block_count], rest[block_count]
    pairs, pair_width, wide = queries.shape
    half, cells = pair_width // 2, wide // 2
    rows = [block[...].astype(jnp.float32) for block in blocks]
    anchors = jnp.concatenate(rows, axis=0).astype(jnp.bfloat16)
    values = lax.dot_general(
        value_turned[...], anchors, (((1,), (1,)), ((), ())), preferred_element_type=jnp.float32
    ).astype(jnp.bfloat16)
    keys = jnp.dot(anchors, lookup[...], preferred_element_type=jnp.float32).astype(jnp.bfloat16)
    scale = 1.0 / math.sqrt(half)
    spans = [slice(pair * pair_width, (pair + 1) * pair_width) for pair in range(pairs)]
    scores = [
        jnp.dot(keys[:, span], queries[pair], preferred_element_type=jnp.float32)
        for pair, span in enumerate(spans)
    ]
    scores = [score * (multiplier[pair : pair + 1, :] * scale) for pair, score in enumerate(scores)]
    exp_scores = [jnp.exp(score - jnp.max(score, axis=0, keepdims=True)) for score in scores]
    denominators = [jnp.sum(exp_score, axis=0, keepdims=True) for exp_score in exp_scores]
    added = [
        jnp.dot(values[span, :], exp_score.astype(jnp.bfloat16), preferred_element_type=jnp.float32)
        for span, exp_score in zip(spans, exp_scores)
    ]
    context = []
    for pair_added, denominator in zip(added, denominators):
        context.append(pair_added[:half, :cells] / denominator[:, :cells])
        context.append(pair_added[half:, cells:] / denominator[:, cells:])
    terms[...] = lax.dot_general(
        jnp.concatenate(context, axis=0).astype(jnp.bfloat16),
        final[...],
        (((0,), (0,)), ((), ())),
        preferred_element_type=jnp.float32,
    ).astype(jnp.bfloat16)


def finish_kernel(own, other, update):
    mixed = own[...].astype(jnp.float32) + other[...].astype(jnp.float32)
    factor = lax.rsqrt(jnp.mean(mixed * mixed, axis=1, keepdims=True) + epsilon)
    width = update.shape[1]
    for part in range(mixed.shape[1] // width):

        @pl.when(lax.axis_index("head") == part)
        def _():
            update[...] = (mixed[:, part * width : (part + 1) * width] * factor).astype(update.dtype)


VMEM = pl.BlockSpec(memory_space=pltpu.VMEM)
HBM = pl.BlockSpec(memory_space=pltpu.HBM)
PARAMS = pltpu.CompilerParams(vmem_limit_bytes=32 * 1024 * 1024)


SEARCHED_ROUNDS = [
    (2, 7, 11, 8, 9, 6, 10, 13, 5, 14, 15, 0, 4, 3, 12, 1),
    (8, 11, 15, 4, 13, 2, 14, 9, 0, 3, 7, 12, 10, 1, 6, 5),
    (5, 12, 7, 0, 11, 14, 1, 2, 13, 6, 4, 9, 8, 15, 3, 10),
    (14, 15, 13, 12, 0, 1, 4, 5, 10, 11, 3, 2, 6, 7, 9, 8),
]


def permute_rounds(shards):
    if 2 * shards == len(SEARCHED_ROUNDS[0]):
        return SEARCHED_ROUNDS
    hops = [(hop + 1, hop) for hop in range(1, shards - 1, 2)] + [(shards - 1, shards - 1)]
    return [
        tuple(2 * ((t + pair[core]) % shards) + core for t in range(shards) for core in (0, 1))
        for pair in hops
    ]


def direct_body(
    shards,
    interior_element_embedding,
    boundary_element_embedding,
    interior_landmark_position,
    boundary_landmark_position,
    interior_rescaling_factor,
    boundary_rescaling_factor,
    question_projection_matrix,
    lookup_projection_matrix,
    content_projection_matrix,
    final_projection_matrix,
    channel_logit_divisor,
):
    cells, width = interior_element_embedding.shape
    local_width = question_projection_matrix.shape[1]
    heads = channel_logit_divisor.shape[0]
    pair_width = 2 * (local_width // heads)
    picks = interior_landmark_position.shape[0] + boundary_landmark_position.shape[0]
    anchors, vol, vol_gain, multiplier = pl.pallas_call(
        anchor_kernel,
        out_shape=(
            jax.ShapeDtypeStruct((picks, width), jnp.bfloat16),
            jax.ShapeDtypeStruct((cells, width), jnp.bfloat16),
            jax.ShapeDtypeStruct((1, width), jnp.float32),
            jax.ShapeDtypeStruct((heads // 2, 2 * cells), jnp.float32),
        ),
        in_specs=[HBM] * 7,
        out_specs=(VMEM,) * 4,
        scratch_shapes=[
            pltpu.SMEM(interior_landmark_position.shape, jnp.int32),
            pltpu.SMEM(boundary_landmark_position.shape, jnp.int32),
            pltpu.VMEM(boundary_element_embedding.shape, jnp.bfloat16),
            pltpu.VMEM((1, width), jnp.float32),
            pltpu.SMEM((heads,), jnp.float32),
            pltpu.SemaphoreType.DMA((7,)),
        ],
        compiler_params=PARAMS,
        name="anchors",
    )(
        *in_hbm(
            interior_landmark_position,
            boundary_landmark_position,
            interior_element_embedding,
            boundary_element_embedding,
            interior_rescaling_factor.reshape(1, width),
            boundary_rescaling_factor.reshape(1, width),
            channel_logit_divisor,
        )
    )
    rounds = permute_rounds(shards)
    again = pl.pallas_call(
        copy_kernel,
        out_shape=jax.ShapeDtypeStruct(anchors.shape, anchors.dtype),
        in_specs=[VMEM],
        out_specs=VMEM,
        compiler_params=PARAMS,
        cost_estimate=pl.CostEstimate(flops=2 * 10**10, bytes_accessed=2**16, transcendentals=0),
        name="again",
    )(*in_vmem(anchors))
    arrived = [
        lax.ppermute(sent, ("tok", "head"), list(enumerate(targets)))
        for sent, targets in [(again, rounds[-1])] + [(anchors, targets) for targets in rounds[:-1]]
    ]
    queries, value_turned = pl.pallas_call(
        query_kernel,
        out_shape=(
            jax.ShapeDtypeStruct((heads // 2, pair_width, 2 * cells), jnp.bfloat16),
            jax.ShapeDtypeStruct((local_width, width), jnp.bfloat16),
        ),
        in_specs=[VMEM] * 6,
        out_specs=(VMEM, VMEM),
        compiler_params=PARAMS,
        cost_estimate=pl.CostEstimate(
            flops=2 * cells * width * local_width, bytes_accessed=8 * width * local_width, transcendentals=0
        ),
        name="queries",
    )(*in_vmem(vol, vol_gain, question_projection_matrix, content_projection_matrix, lookup_projection_matrix, final_projection_matrix))
    swapped = [lax.ppermute(block, "head", [(0, 1), (1, 0)]) for block in arrived[1:]]
    blocks = [anchors, *arrived, *swapped]
    terms = pl.pallas_call(
        functools.partial(attention_kernel, len(blocks)),
        out_shape=jax.ShapeDtypeStruct((cells, width), jnp.bfloat16),
        in_specs=[VMEM] * (5 + len(blocks)),
        out_specs=VMEM,
        compiler_params=PARAMS,
        name="attention",
    )(
        *in_vmem(queries, multiplier, lookup_projection_matrix, value_turned, final_projection_matrix, *blocks),
    )
    other = lax.ppermute(terms, "head", [(0, 1), (1, 0)])
    return pl.pallas_call(
        finish_kernel,
        out_shape=jax.ShapeDtypeStruct((cells, local_width), jnp.bfloat16),
        in_specs=[VMEM, VMEM],
        out_specs=VMEM,
        compiler_params=PARAMS,
        name="finish",
    )(*in_vmem(terms, other))


def solution(mesh):
    placed = (
        P(("groups", "tok"), None),
        P(("groups", "tok"), None),
        P(("groups", "tok")),
        P(("groups", "tok")),
        P(),
        P(),
        P(None, "head"),
        P(None, "head"),
        P(None, "head"),
        P("head", None),
        P("head"),
    )
    shards = mesh.shape["tok"]
    small = shards % 2 == 0 and shards <= 16 and mesh.shape["head"] == 2
    body = functools.partial(direct_body, shards) if small else gathered_body
    return jax.shard_map(
        body, mesh=mesh, in_specs=placed, out_specs=P(("groups", "tok"), "head"), check_vma=False
    )
```

```python
import functools
import math

import jax
import jax.numpy as jnp
from jax import lax
from jax.experimental import pallas as pl
from jax.experimental.pallas import tpu as pltpu
from jax.sharding import PartitionSpec as P

epsilon = 1e-06
key_block = 512


def rms_rows(cells, gain):
    values = cells.astype(jnp.float32)
    mean_square = jnp.mean(values * values, axis=1, keepdims=True)
    return (values * lax.rsqrt(mean_square + epsilon) * gain).astype(jnp.bfloat16)


def absorb(running, key_rows, value_rows, queries, logit_multiplier):
    run_max, denominator, accumulated = running
    parallel_channel_total, channel_dimension, cell_count = queries.shape
    key_heads = key_rows.reshape(key_rows.shape[0], parallel_channel_total, channel_dimension)
    value_heads = value_rows.reshape(value_rows.shape[0], parallel_channel_total, channel_dimension)
    scores = (
        jnp.einsum("jhd,hdc->hjc", key_heads, queries, preferred_element_type=jnp.float32)
        * logit_multiplier
    )
    new_max = jnp.maximum(run_max, jnp.max(scores, axis=1))
    shrink = jnp.exp(run_max - new_max)
    exp_scores = jnp.exp(scores - new_max[:, None, :])
    denominator = denominator * shrink + jnp.sum(exp_scores, axis=1)
    added = jnp.einsum(
        "jhd,hjc->hdc",
        value_heads,
        exp_scores.astype(jnp.bfloat16),
        preferred_element_type=jnp.float32,
    )
    accumulated = accumulated * shrink[:, None, :] + added
    return (new_max, denominator, accumulated)


def make_folder(queries, logit_multiplier):

    def folder(running, shard_rows, offset):
        key_rows, value_rows = shard_rows
        row_count = key_rows.shape[0]
        if row_count > key_block and row_count % key_block == 0:
            row_width = key_rows.shape[1]

            def scan_step(state, key_pair):
                return (absorb(state, key_pair[0], key_pair[1], queries, logit_multiplier), None)

            stacked = (
                key_rows.reshape(row_count // key_block, key_block, row_width),
                value_rows.reshape(row_count // key_block, key_block, row_width),
            )
            running, unused = lax.scan(scan_step, running, stacked)
            return running
        return absorb(running, key_rows, value_rows, queries, logit_multiplier)

    return folder


def project_pair(rows_in, lookup_projection_matrix, content_projection_matrix):
    key_rows = jnp.dot(
        rows_in, lookup_projection_matrix, preferred_element_type=jnp.float32
    ).astype(jnp.bfloat16)
    value_rows = jnp.dot(
        rows_in, content_projection_matrix, preferred_element_type=jnp.float32
    ).astype(jnp.bfloat16)
    return (key_rows, value_rows)


def gathered_body(
    interior_element_embedding,
    boundary_element_embedding,
    interior_landmark_position,
    boundary_landmark_position,
    interior_rescaling_factor,
    boundary_rescaling_factor,
    question_projection_matrix,
    lookup_projection_matrix,
    content_projection_matrix,
    final_projection_matrix,
    channel_logit_divisor,
):
    block_index = lax.axis_index("tok")
    vol_normed = rms_rows(interior_element_embedding, interior_rescaling_factor)
    vol_local = interior_landmark_position - block_index * interior_element_embedding.shape[0]
    surf_local = boundary_landmark_position - block_index * boundary_element_embedding.shape[0]
    vol_picked = jnp.take(vol_normed, vol_local, axis=0)
    surf_picked = rms_rows(
        jnp.take(boundary_element_embedding, surf_local, axis=0), boundary_rescaling_factor
    )
    parallel_channel_total = channel_logit_divisor.shape[0]
    local_width = question_projection_matrix.shape[1]
    channel_dimension = local_width // parallel_channel_total
    cell_count = interior_element_embedding.shape[0]
    query_cols = lax.dot_general(
        question_projection_matrix,
        vol_normed,
        (((0,), (1,)), ((), ())),
        preferred_element_type=jnp.float32,
    )
    queries = query_cols.astype(jnp.bfloat16).reshape(
        parallel_channel_total, channel_dimension, cell_count
    )
    logit_multiplier = (channel_logit_divisor * (1.0 / math.sqrt(channel_dimension)))[:, None, None]
    start_state = (
        jnp.full((parallel_channel_total, cell_count), -1e30, jnp.float32),
        jnp.zeros((parallel_channel_total, cell_count), jnp.float32),
        jnp.zeros((parallel_channel_total, channel_dimension, cell_count), jnp.float32),
    )
    folder = make_folder(queries, logit_multiplier)
    anchors = jnp.concatenate([vol_picked, surf_picked], axis=0)
    anchor_keys, anchor_values = project_pair(
        anchors, lookup_projection_matrix, content_projection_matrix
    )
    final_state = folder(
        start_state,
        (
            lax.all_gather(anchor_keys, "tok", axis=0, tiled=True),
            lax.all_gather(anchor_values, "tok", axis=0, tiled=True),
        ),
        jnp.int32(0),
    )
    run_max, denominator, accumulated = final_state
    context = (
        (accumulated / denominator[:, None, :])
        .astype(jnp.bfloat16)
        .reshape(local_width, cell_count)
    )
    head_terms = lax.dot_general(
        context,
        final_projection_matrix,
        (((0,), (0,)), ((), ())),
        preferred_element_type=jnp.float32,
    )
    full_width = head_terms.shape[1]
    share = lax.psum_scatter(
        head_terms.astype(jnp.bfloat16), "head", scatter_dimension=1, tiled=True
    ).astype(jnp.float32)
    squares = lax.psum(jnp.sum(share * share, axis=1), "head")
    return (share * lax.rsqrt(squares[:, None] / full_width + epsilon)).astype(jnp.bfloat16)


def in_vmem(*arrays):
    return [pltpu.with_memory_space_constraint(array, pltpu.VMEM) for array in arrays]


def in_hbm(*arrays):
    return [pltpu.with_memory_space_constraint(array, pltpu.HBM) for array in arrays]


def normed(values, gain):
    mean_square = jnp.mean(values * values, axis=1, keepdims=True)
    return (values * lax.rsqrt(mean_square + epsilon) * gain).astype(jnp.bfloat16)


def pick_rows(positions, first, cells):
    picks, rows = positions.shape[0], cells.shape[0]
    row = lax.broadcasted_iota(jnp.int32, (picks, rows), 0)
    column = lax.broadcasted_iota(jnp.int32, (picks, rows), 1)
    chosen = jnp.zeros((picks, rows), jnp.int32)
    for pick in range(picks):
        chosen = jnp.where(row == pick, positions[pick] - first, chosen)
    one_hot = jnp.where(chosen == column, 1.0, 0.0).astype(jnp.bfloat16)
    return jnp.dot(one_hot, cells, preferred_element_type=jnp.float32)


def fetch(sources, targets, semaphores):
    copies = [
        pltpu.make_async_copy(source, target, semaphores.at[number])
        for number, (source, target) in enumerate(zip(sources, targets))
    ]
    for copy in copies:
        copy.start()
    return copies


def anchor_kernel(*refs):
    sources, (anchors, vol, vol_gain, multiplier), rest = refs[:7], refs[7:11], refs[11:]
    vol_position, surf_position, surf, surf_gain, divisor, semaphores = rest
    targets = (vol_position, surf_position, vol, surf, vol_gain, surf_gain, divisor)
    for copy in fetch(sources, targets, semaphores):
        copy.wait()
    block_index = lax.axis_index("tok")
    vol_rows = pick_rows(vol_position, block_index * vol.shape[0], vol[...])
    surf_rows = pick_rows(surf_position, block_index * surf.shape[0], surf[...])
    parts = [normed(vol_rows, vol_gain[...]), normed(surf_rows, surf_gain[...])]
    stacked = jnp.concatenate([part.astype(jnp.float32) for part in parts], axis=0)
    anchors[...] = stacked.astype(jnp.bfloat16)
    pairs, wide = multiplier.shape
    left = lax.broadcasted_iota(jnp.int32, (1, wide), 1) < wide // 2
    for pair in range(pairs):
        multiplier[pair : pair + 1, :] = jnp.where(left, divisor[2 * pair], divisor[2 * pair + 1])


def copy_kernel(source, target):
    target[...] = source[...]


def query_kernel(vol, gain, projection, value_projection, lookup, final, queries, value_turned):
    vol_normed = normed(vol[...].astype(jnp.float32), gain[...])
    cells = vol.shape[0]
    columns = lax.dot_general(
        projection[...], vol_normed, (((0,), (1,)), ((), ())), preferred_element_type=jnp.float32
    ).astype(jnp.bfloat16)
    pairs, pair_width, _ = queries.shape
    upper = lax.broadcasted_iota(jnp.int32, (pair_width, cells), 0) < pair_width // 2
    for pair in range(pairs):
        block = columns[pair * pair_width : (pair + 1) * pair_width, :].astype(jnp.float32)
        queries[pair, :, :cells] = jnp.where(upper, block, 0.0).astype(jnp.bfloat16)
        queries[pair, :, cells:] = jnp.where(upper, 0.0, block).astype(jnp.bfloat16)
    value_turned[...] = value_projection[...].T


def attention_kernel(block_count, queries, multiplier, lookup, value_turned, final, *rest):
    blocks, terms = rest[:block_count], rest[block_count]
    pairs, pair_width, wide = queries.shape
    half, cells = pair_width // 2, wide // 2
    rows = [block[...].astype(jnp.float32) for block in blocks]
    anchors = jnp.concatenate(rows, axis=0).astype(jnp.bfloat16)
    values = lax.dot_general(
        value_turned[...], anchors, (((1,), (1,)), ((), ())), preferred_element_type=jnp.float32
    ).astype(jnp.bfloat16)
    keys = jnp.dot(anchors, lookup[...], preferred_element_type=jnp.float32).astype(jnp.bfloat16)
    scale = 1.0 / math.sqrt(half)
    spans = [slice(pair * pair_width, (pair + 1) * pair_width) for pair in range(pairs)]
    scores = [
        jnp.dot(keys[:, span], queries[pair], preferred_element_type=jnp.float32)
        for pair, span in enumerate(spans)
    ]
    scores = [score * (multiplier[pair : pair + 1, :] * scale) for pair, score in enumerate(scores)]
    exp_scores = [jnp.exp(score - jnp.max(score, axis=0, keepdims=True)) for score in scores]
    denominators = [jnp.sum(exp_score, axis=0, keepdims=True) for exp_score in exp_scores]
    added = [
        jnp.dot(values[span, :], exp_score.astype(jnp.bfloat16), preferred_element_type=jnp.float32)
        for span, exp_score in zip(spans, exp_scores)
    ]
    context = []
    for pair_added, denominator in zip(added, denominators):
        context.append(pair_added[:half, :cells] / denominator[:, :cells])
        context.append(pair_added[half:, cells:] / denominator[:, cells:])
    terms[...] = lax.dot_general(
        jnp.concatenate(context, axis=0).astype(jnp.bfloat16),
        final[...],
        (((0,), (0,)), ((), ())),
        preferred_element_type=jnp.float32,
    ).astype(jnp.bfloat16)


def finish_kernel(own, other, update):
    mixed = own[...].astype(jnp.float32) + other[...].astype(jnp.float32)
    factor = lax.rsqrt(jnp.mean(mixed * mixed, axis=1, keepdims=True) + epsilon)
    width = update.shape[1]
    for part in range(mixed.shape[1] // width):

        @pl.when(lax.axis_index("head") == part)
        def _():
            update[...] = (mixed[:, part * width : (part + 1) * width] * factor).astype(update.dtype)


VMEM = pl.BlockSpec(memory_space=pltpu.VMEM)
HBM = pl.BlockSpec(memory_space=pltpu.HBM)
PARAMS = pltpu.CompilerParams(vmem_limit_bytes=32 * 1024 * 1024)


SEARCHED_ROUNDS = [
    (2, 7, 11, 8, 9, 6, 10, 13, 5, 14, 15, 0, 4, 3, 12, 1),
    (8, 11, 15, 4, 13, 2, 14, 9, 0, 3, 7, 12, 10, 1, 6, 5),
    (5, 12, 7, 0, 11, 14, 1, 2, 13, 6, 4, 9, 15, 8, 3, 10),
    (14, 15, 13, 12, 0, 1, 4, 5, 10, 11, 3, 2, 6, 7, 9, 8),
]


def permute_rounds(shards):
    if 2 * shards == len(SEARCHED_ROUNDS[0]):
        return SEARCHED_ROUNDS
    hops = [(hop + 1, hop) for hop in range(1, shards - 1, 2)] + [(shards - 1, shards - 1)]
    return [
        tuple(2 * ((t + pair[core]) % shards) + core for t in range(shards) for core in (0, 1))
        for pair in hops
    ]


def direct_body(
    shards,
    interior_element_embedding,
    boundary_element_embedding,
    interior_landmark_position,
    boundary_landmark_position,
    interior_rescaling_factor,
    boundary_rescaling_factor,
    question_projection_matrix,
    lookup_projection_matrix,
    content_projection_matrix,
    final_projection_matrix,
    channel_logit_divisor,
):
    cells, width = interior_element_embedding.shape
    local_width = question_projection_matrix.shape[1]
    heads = channel_logit_divisor.shape[0]
    pair_width = 2 * (local_width // heads)
    picks = interior_landmark_position.shape[0] + boundary_landmark_position.shape[0]
    anchors, vol, vol_gain, multiplier = pl.pallas_call(
        anchor_kernel,
        out_shape=(
            jax.ShapeDtypeStruct((picks, width), jnp.bfloat16),
            jax.ShapeDtypeStruct((cells, width), jnp.bfloat16),
            jax.ShapeDtypeStruct((1, width), jnp.float32),
            jax.ShapeDtypeStruct((heads // 2, 2 * cells), jnp.float32),
        ),
        in_specs=[HBM] * 7,
        out_specs=(VMEM,) * 4,
        scratch_shapes=[
            pltpu.SMEM(interior_landmark_position.shape, jnp.int32),
            pltpu.SMEM(boundary_landmark_position.shape, jnp.int32),
            pltpu.VMEM(boundary_element_embedding.shape, jnp.bfloat16),
            pltpu.VMEM((1, width), jnp.float32),
            pltpu.SMEM((heads,), jnp.float32),
            pltpu.SemaphoreType.DMA((7,)),
        ],
        compiler_params=PARAMS,
        name="anchors",
    )(
        *in_hbm(
            interior_landmark_position,
            boundary_landmark_position,
            interior_element_embedding,
            boundary_element_embedding,
            interior_rescaling_factor.reshape(1, width),
            boundary_rescaling_factor.reshape(1, width),
            channel_logit_divisor,
        )
    )
    rounds = permute_rounds(shards)
    again = pl.pallas_call(
        copy_kernel,
        out_shape=jax.ShapeDtypeStruct(anchors.shape, anchors.dtype),
        in_specs=[VMEM],
        out_specs=VMEM,
        compiler_params=PARAMS,
        cost_estimate=pl.CostEstimate(flops=2 * 10**10, bytes_accessed=2**16, transcendentals=0),
        name="again",
    )(*in_vmem(anchors))
    arrived = [
        lax.ppermute(sent, ("tok", "head"), list(enumerate(targets)))
        for sent, targets in [(again, rounds[-1])] + [(anchors, targets) for targets in rounds[:-1]]
    ]
    queries, value_turned = pl.pallas_call(
        query_kernel,
        out_shape=(
            jax.ShapeDtypeStruct((heads // 2, pair_width, 2 * cells), jnp.bfloat16),
            jax.ShapeDtypeStruct((local_width, width), jnp.bfloat16),
        ),
        in_specs=[VMEM] * 6,
        out_specs=(VMEM, VMEM),
        compiler_params=PARAMS,
        cost_estimate=pl.CostEstimate(
            flops=2 * cells * width * local_width, bytes_accessed=8 * width * local_width, transcendentals=0
        ),
        name="queries",
    )(*in_vmem(vol, vol_gain, question_projection_matrix, content_projection_matrix, lookup_projection_matrix, final_projection_matrix))
    swapped = [lax.ppermute(block, "head", [(0, 1), (1, 0)]) for block in arrived[1:]]
    blocks = [anchors, *arrived, *swapped]
    terms = pl.pallas_call(
        functools.partial(attention_kernel, len(blocks)),
        out_shape=jax.ShapeDtypeStruct((cells, width), jnp.bfloat16),
        in_specs=[VMEM] * (5 + len(blocks)),
        out_specs=VMEM,
        compiler_params=PARAMS,
        name="attention",
    )(
        *in_vmem(queries, multiplier, lookup_projection_matrix, value_turned, final_projection_matrix, *blocks),
    )
    other = lax.ppermute(terms, "head", [(0, 1), (1, 0)])
    return pl.pallas_call(
        finish_kernel,
        out_shape=jax.ShapeDtypeStruct((cells, local_width), jnp.bfloat16),
        in_specs=[VMEM, VMEM],
        out_specs=VMEM,
        compiler_params=PARAMS,
        name="finish",
    )(*in_vmem(terms, other))


def solution(mesh):
    placed = (
        P(("groups", "tok"), None),
        P(("groups", "tok"), None),
        P(("groups", "tok")),
        P(("groups", "tok")),
        P(),
        P(),
        P(None, "head"),
        P(None, "head"),
        P(None, "head"),
        P("head", None),
        P("head"),
    )
    shards = mesh.shape["tok"]
    small = shards % 2 == 0 and shards <= 16 and mesh.shape["head"] == 2
    body = functools.partial(direct_body, shards) if small else gathered_body
    return jax.shard_map(
        body, mesh=mesh, in_specs=placed, out_specs=P(("groups", "tok"), "head"), check_vma=False
    )
```

```python
import functools
import math

import jax
import jax.numpy as jnp
from jax import lax
from jax.experimental import pallas as pl
from jax.experimental.pallas import tpu as pltpu
from jax.sharding import PartitionSpec as P

epsilon = 1e-06
key_block = 512


def rms_rows(cells, gain):
    values = cells.astype(jnp.float32)
    mean_square = jnp.mean(values * values, axis=1, keepdims=True)
    return (values * lax.rsqrt(mean_square + epsilon) * gain).astype(jnp.bfloat16)


def absorb(running, key_rows, value_rows, queries, logit_multiplier):
    run_max, denominator, accumulated = running
    parallel_channel_total, channel_dimension, cell_count = queries.shape
    key_heads = key_rows.reshape(key_rows.shape[0], parallel_channel_total, channel_dimension)
    value_heads = value_rows.reshape(value_rows.shape[0], parallel_channel_total, channel_dimension)
    scores = (
        jnp.einsum("jhd,hdc->hjc", key_heads, queries, preferred_element_type=jnp.float32)
        * logit_multiplier
    )
    new_max = jnp.maximum(run_max, jnp.max(scores, axis=1))
    shrink = jnp.exp(run_max - new_max)
    exp_scores = jnp.exp(scores - new_max[:, None, :])
    denominator = denominator * shrink + jnp.sum(exp_scores, axis=1)
    added = jnp.einsum(
        "jhd,hjc->hdc",
        value_heads,
        exp_scores.astype(jnp.bfloat16),
        preferred_element_type=jnp.float32,
    )
    accumulated = accumulated * shrink[:, None, :] + added
    return (new_max, denominator, accumulated)


def make_folder(queries, logit_multiplier):

    def folder(running, shard_rows, offset):
        key_rows, value_rows = shard_rows
        row_count = key_rows.shape[0]
        if row_count > key_block and row_count % key_block == 0:
            row_width = key_rows.shape[1]

            def scan_step(state, key_pair):
                return (absorb(state, key_pair[0], key_pair[1], queries, logit_multiplier), None)

            stacked = (
                key_rows.reshape(row_count // key_block, key_block, row_width),
                value_rows.reshape(row_count // key_block, key_block, row_width),
            )
            running, unused = lax.scan(scan_step, running, stacked)
            return running
        return absorb(running, key_rows, value_rows, queries, logit_multiplier)

    return folder


def project_pair(rows_in, lookup_projection_matrix, content_projection_matrix):
    key_rows = jnp.dot(
        rows_in, lookup_projection_matrix, preferred_element_type=jnp.float32
    ).astype(jnp.bfloat16)
    value_rows = jnp.dot(
        rows_in, content_projection_matrix, preferred_element_type=jnp.float32
    ).astype(jnp.bfloat16)
    return (key_rows, value_rows)


def gathered_body(
    interior_element_embedding,
    boundary_element_embedding,
    interior_landmark_position,
    boundary_landmark_position,
    interior_rescaling_factor,
    boundary_rescaling_factor,
    question_projection_matrix,
    lookup_projection_matrix,
    content_projection_matrix,
    final_projection_matrix,
    channel_logit_divisor,
):
    block_index = lax.axis_index("tok")
    vol_normed = rms_rows(interior_element_embedding, interior_rescaling_factor)
    vol_local = interior_landmark_position - block_index * interior_element_embedding.shape[0]
    surf_local = boundary_landmark_position - block_index * boundary_element_embedding.shape[0]
    vol_picked = jnp.take(vol_normed, vol_local, axis=0)
    surf_picked = rms_rows(
        jnp.take(boundary_element_embedding, surf_local, axis=0), boundary_rescaling_factor
    )
    parallel_channel_total = channel_logit_divisor.shape[0]
    local_width = question_projection_matrix.shape[1]
    channel_dimension = local_width // parallel_channel_total
    cell_count = interior_element_embedding.shape[0]
    query_cols = lax.dot_general(
        question_projection_matrix,
        vol_normed,
        (((0,), (1,)), ((), ())),
        preferred_element_type=jnp.float32,
    )
    queries = query_cols.astype(jnp.bfloat16).reshape(
        parallel_channel_total, channel_dimension, cell_count
    )
    logit_multiplier = (channel_logit_divisor * (1.0 / math.sqrt(channel_dimension)))[:, None, None]
    start_state = (
        jnp.full((parallel_channel_total, cell_count), -1e30, jnp.float32),
        jnp.zeros((parallel_channel_total, cell_count), jnp.float32),
        jnp.zeros((parallel_channel_total, channel_dimension, cell_count), jnp.float32),
    )
    folder = make_folder(queries, logit_multiplier)
    anchors = jnp.concatenate([vol_picked, surf_picked], axis=0)
    anchor_keys, anchor_values = project_pair(
        anchors, lookup_projection_matrix, content_projection_matrix
    )
    final_state = folder(
        start_state,
        (
            lax.all_gather(anchor_keys, "tok", axis=0, tiled=True),
            lax.all_gather(anchor_values, "tok", axis=0, tiled=True),
        ),
        jnp.int32(0),
    )
    run_max, denominator, accumulated = final_state
    context = (
        (accumulated / denominator[:, None, :])
        .astype(jnp.bfloat16)
        .reshape(local_width, cell_count)
    )
    head_terms = lax.dot_general(
        context,
        final_projection_matrix,
        (((0,), (0,)), ((), ())),
        preferred_element_type=jnp.float32,
    )
    full_width = head_terms.shape[1]
    share = lax.psum_scatter(
        head_terms.astype(jnp.bfloat16), "head", scatter_dimension=1, tiled=True
    ).astype(jnp.float32)
    squares = lax.psum(jnp.sum(share * share, axis=1), "head")
    return (share * lax.rsqrt(squares[:, None] / full_width + epsilon)).astype(jnp.bfloat16)


def in_vmem(*arrays):
    return [pltpu.with_memory_space_constraint(array, pltpu.VMEM) for array in arrays]


def in_hbm(*arrays):
    return [pltpu.with_memory_space_constraint(array, pltpu.HBM) for array in arrays]


def normed(values, gain):
    mean_square = jnp.mean(values * values, axis=1, keepdims=True)
    return (values * lax.rsqrt(mean_square + epsilon) * gain).astype(jnp.bfloat16)


def pick_rows(positions, first, cells):
    picks, rows = positions.shape[0], cells.shape[0]
    row = lax.broadcasted_iota(jnp.int32, (picks, rows), 0)
    column = lax.broadcasted_iota(jnp.int32, (picks, rows), 1)
    chosen = jnp.zeros((picks, rows), jnp.int32)
    for pick in range(picks):
        chosen = jnp.where(row == pick, positions[pick] - first, chosen)
    one_hot = jnp.where(chosen == column, 1.0, 0.0).astype(jnp.bfloat16)
    return jnp.dot(one_hot, cells, preferred_element_type=jnp.float32)


def fetch(sources, targets, semaphores):
    copies = [
        pltpu.make_async_copy(source, target, semaphores.at[number])
        for number, (source, target) in enumerate(zip(sources, targets))
    ]
    for copy in copies:
        copy.start()
    return copies


def anchor_kernel(*refs):
    sources, (anchors, vol, vol_gain, multiplier), rest = refs[:7], refs[7:11], refs[11:]
    vol_position, surf_position, surf, surf_gain, divisor, semaphores = rest
    targets = (vol, surf, vol_position, surf_position, vol_gain, surf_gain, divisor)
    for copy in fetch(sources, targets, semaphores):
        copy.wait()
    block_index = lax.axis_index("tok")
    vol_rows = pick_rows(vol_position, block_index * vol.shape[0], vol[...])
    surf_rows = pick_rows(surf_position, block_index * surf.shape[0], surf[...])
    parts = [normed(vol_rows, vol_gain[...]), normed(surf_rows, surf_gain[...])]
    stacked = jnp.concatenate([part.astype(jnp.float32) for part in parts], axis=0)
    anchors[...] = stacked.astype(jnp.bfloat16)
    pairs, wide = multiplier.shape
    left = lax.broadcasted_iota(jnp.int32, (1, wide), 1) < wide // 2
    for pair in range(pairs):
        multiplier[pair : pair + 1, :] = jnp.where(left, divisor[2 * pair], divisor[2 * pair + 1])


def copy_kernel(source, target):
    target[...] = source[...]


def query_kernel(vol, gain, projection, value_projection, lookup, final, queries, value_turned):
    vol_normed = normed(vol[...].astype(jnp.float32), gain[...])
    cells = vol.shape[0]
    columns = lax.dot_general(
        projection[...], vol_normed, (((0,), (1,)), ((), ())), preferred_element_type=jnp.float32
    ).astype(jnp.bfloat16)
    pairs, pair_width, _ = queries.shape
    upper = lax.broadcasted_iota(jnp.int32, (pair_width, cells), 0) < pair_width // 2
    for pair in range(pairs):
        block = columns[pair * pair_width : (pair + 1) * pair_width, :].astype(jnp.float32)
        queries[pair, :, :cells] = jnp.where(upper, block, 0.0).astype(jnp.bfloat16)
        queries[pair, :, cells:] = jnp.where(upper, 0.0, block).astype(jnp.bfloat16)
    value_turned[...] = value_projection[...].T


def attention_kernel(block_count, queries, multiplier, lookup, value_turned, final, *rest):
    blocks, terms = rest[:block_count], rest[block_count]
    pairs, pair_width, wide = queries.shape
    half, cells = pair_width // 2, wide // 2
    rows = [block[...].astype(jnp.float32) for block in blocks]
    anchors = jnp.concatenate(rows, axis=0).astype(jnp.bfloat16)
    values = lax.dot_general(
        value_turned[...], anchors, (((1,), (1,)), ((), ())), preferred_element_type=jnp.float32
    ).astype(jnp.bfloat16)
    keys = jnp.dot(anchors, lookup[...], preferred_element_type=jnp.float32).astype(jnp.bfloat16)
    scale = 1.0 / math.sqrt(half)
    spans = [slice(pair * pair_width, (pair + 1) * pair_width) for pair in range(pairs)]
    scores = [
        jnp.dot(keys[:, span], queries[pair], preferred_element_type=jnp.float32)
        for pair, span in enumerate(spans)
    ]
    scores = [score * (multiplier[pair : pair + 1, :] * scale) for pair, score in enumerate(scores)]
    exp_scores = [jnp.exp(score - jnp.max(score, axis=0, keepdims=True)) for score in scores]
    denominators = [jnp.sum(exp_score, axis=0, keepdims=True) for exp_score in exp_scores]
    added = [
        jnp.dot(values[span, :], exp_score.astype(jnp.bfloat16), preferred_element_type=jnp.float32)
        for span, exp_score in zip(spans, exp_scores)
    ]
    context = []
    for pair_added, denominator in zip(added, denominators):
        context.append(pair_added[:half, :cells] / denominator[:, :cells])
        context.append(pair_added[half:, cells:] / denominator[:, cells:])
    terms[...] = lax.dot_general(
        jnp.concatenate(context, axis=0).astype(jnp.bfloat16),
        final[...],
        (((0,), (0,)), ((), ())),
        preferred_element_type=jnp.float32,
    ).astype(jnp.bfloat16)


def finish_kernel(own, other, update):
    mixed = own[...].astype(jnp.float32) + other[...].astype(jnp.float32)
    factor = lax.rsqrt(jnp.mean(mixed * mixed, axis=1, keepdims=True) + epsilon)
    width = update.shape[1]
    for part in range(mixed.shape[1] // width):

        @pl.when(lax.axis_index("head") == part)
        def _():
            update[...] = (mixed[:, part * width : (part + 1) * width] * factor).astype(update.dtype)


VMEM = pl.BlockSpec(memory_space=pltpu.VMEM)
HBM = pl.BlockSpec(memory_space=pltpu.HBM)
PARAMS = pltpu.CompilerParams(vmem_limit_bytes=32 * 1024 * 1024)


SEARCHED_ROUNDS = [
    (2, 7, 11, 8, 9, 6, 10, 13, 5, 14, 15, 0, 4, 3, 12, 1),
    (8, 11, 15, 4, 13, 2, 14, 9, 0, 3, 7, 12, 10, 1, 6, 5),
    (5, 12, 7, 0, 11, 14, 1, 2, 13, 6, 4, 9, 15, 8, 3, 10),
    (14, 15, 13, 12, 0, 1, 4, 5, 10, 11, 3, 2, 6, 7, 9, 8),
]


def permute_rounds(shards):
    if 2 * shards == len(SEARCHED_ROUNDS[0]):
        return SEARCHED_ROUNDS
    hops = [(hop + 1, hop) for hop in range(1, shards - 1, 2)] + [(shards - 1, shards - 1)]
    return [
        tuple(2 * ((t + pair[core]) % shards) + core for t in range(shards) for core in (0, 1))
        for pair in hops
    ]


def direct_body(
    shards,
    interior_element_embedding,
    boundary_element_embedding,
    interior_landmark_position,
    boundary_landmark_position,
    interior_rescaling_factor,
    boundary_rescaling_factor,
    question_projection_matrix,
    lookup_projection_matrix,
    content_projection_matrix,
    final_projection_matrix,
    channel_logit_divisor,
):
    cells, width = interior_element_embedding.shape
    local_width = question_projection_matrix.shape[1]
    heads = channel_logit_divisor.shape[0]
    pair_width = 2 * (local_width // heads)
    picks = interior_landmark_position.shape[0] + boundary_landmark_position.shape[0]
    anchors, vol, vol_gain, multiplier = pl.pallas_call(
        anchor_kernel,
        out_shape=(
            jax.ShapeDtypeStruct((picks, width), jnp.bfloat16),
            jax.ShapeDtypeStruct((cells, width), jnp.bfloat16),
            jax.ShapeDtypeStruct((1, width), jnp.float32),
            jax.ShapeDtypeStruct((heads // 2, 2 * cells), jnp.float32),
        ),
        in_specs=[HBM] * 7,
        out_specs=(VMEM,) * 4,
        scratch_shapes=[
            pltpu.SMEM(interior_landmark_position.shape, jnp.int32),
            pltpu.SMEM(boundary_landmark_position.shape, jnp.int32),
            pltpu.VMEM(boundary_element_embedding.shape, jnp.bfloat16),
            pltpu.VMEM((1, width), jnp.float32),
            pltpu.SMEM((heads,), jnp.float32),
            pltpu.SemaphoreType.DMA((7,)),
        ],
        compiler_params=PARAMS,
        name="anchors",
    )(
        *in_hbm(
            interior_element_embedding,
            boundary_element_embedding,
            interior_landmark_position,
            boundary_landmark_position,
            interior_rescaling_factor.reshape(1, width),
            boundary_rescaling_factor.reshape(1, width),
            channel_logit_divisor,
        )
    )
    rounds = permute_rounds(shards)
    again = pl.pallas_call(
        copy_kernel,
        out_shape=jax.ShapeDtypeStruct(anchors.shape, anchors.dtype),
        in_specs=[VMEM],
        out_specs=VMEM,
        compiler_params=PARAMS,
        cost_estimate=pl.CostEstimate(flops=2 * 10**10, bytes_accessed=2**16, transcendentals=0),
        name="again",
    )(*in_vmem(anchors))
    arrived = [
        lax.ppermute(sent, ("tok", "head"), list(enumerate(targets)))
        for sent, targets in [(again, rounds[-1])] + [(anchors, targets) for targets in rounds[:-1]]
    ]
    queries, value_turned = pl.pallas_call(
        query_kernel,
        out_shape=(
            jax.ShapeDtypeStruct((heads // 2, pair_width, 2 * cells), jnp.bfloat16),
            jax.ShapeDtypeStruct((local_width, width), jnp.bfloat16),
        ),
        in_specs=[VMEM] * 6,
        out_specs=(VMEM, VMEM),
        compiler_params=PARAMS,
        cost_estimate=pl.CostEstimate(
            flops=2 * cells * width * local_width, bytes_accessed=8 * width * local_width, transcendentals=0
        ),
        name="queries",
    )(*in_vmem(vol, vol_gain, question_projection_matrix, content_projection_matrix, lookup_projection_matrix, final_projection_matrix))
    swapped = [lax.ppermute(block, "head", [(0, 1), (1, 0)]) for block in arrived[1:]]
    blocks = [anchors, *arrived, *swapped]
    terms = pl.pallas_call(
        functools.partial(attention_kernel, len(blocks)),
        out_shape=jax.ShapeDtypeStruct((cells, width), jnp.bfloat16),
        in_specs=[VMEM] * (5 + len(blocks)),
        out_specs=VMEM,
        compiler_params=PARAMS,
        name="attention",
    )(
        *in_vmem(queries, multiplier, lookup_projection_matrix, value_turned, final_projection_matrix, *blocks),
    )
    other = lax.ppermute(terms, "head", [(0, 1), (1, 0)])
    return pl.pallas_call(
        finish_kernel,
        out_shape=jax.ShapeDtypeStruct((cells, local_width), jnp.bfloat16),
        in_specs=[VMEM, VMEM],
        out_specs=VMEM,
        compiler_params=PARAMS,
        name="finish",
    )(*in_vmem(terms, other))


def solution(mesh):
    placed = (
        P(("groups", "tok"), None),
        P(("groups", "tok"), None),
        P(("groups", "tok")),
        P(("groups", "tok")),
        P(),
        P(),
        P(None, "head"),
        P(None, "head"),
        P(None, "head"),
        P("head", None),
        P("head"),
    )
    shards = mesh.shape["tok"]
    small = shards % 2 == 0 and shards <= 16 and mesh.shape["head"] == 2
    body = functools.partial(direct_body, shards) if small else gathered_body
    return jax.shard_map(
        body, mesh=mesh, in_specs=placed, out_specs=P(("groups", "tok"), "head"), check_vma=False
    )
```
